32 devices in a mesh: ctx: 1, exp: 16 (over z, y, x), rep: 2 (over core).
Axes of the slice: x: 2, y: 2, z: 4, core: 2. Of those that a mesh axis runs over, the one named last changes fastest.
Arguments:
- hidden_in: bfloat16 [1024, 4096], P(('rep', 'ctx', 'exp')), parts along dimension 0, may hold values from -6 to 6
- queries: bfloat16 [1024, 8192], P(('rep', 'ctx'), 'exp'), parts along dimension 0, may hold values from -64 to 64
- keys: bfloat16 [1024, 512], P(('rep', 'ctx')), parts along dimension 0, may hold values from -8 to 8
- values: bfloat16 [1024, 512], P(('rep', 'ctx')), parts along dimension 0, may hold values from -6 to 6
- out_proj: bfloat16 [8192, 4096], P('exp'), may hold values from -0.0625 to 0.0625
- norm_gain: float32 [4096], replicated, may hold values from 0.1 to 1.9
- expert_ids: int32 [1024, 8], P(('rep', 'ctx', 'exp')), parts along dimension 0, may hold values from 0 to 127, all different within a row; in each aligned block of 32 rows (0 to 31, 32 to 63, ...) at most 2 rows name the same one
- gate_fixed: int32 [1024, 8], P(('rep', 'ctx', 'exp')), parts along dimension 0, may hold values from 1 to 4096
- live_counts: int32 [32], P(('rep', 'ctx', 'exp')), parts along dimension 0, may hold values from 16 to 32, as said below
- gate_proj: bfloat16 [16, 4096, 1536], P('exp', None, 'ctx'), may hold values from -0.09375 to 0.09375
- up_proj: bfloat16 [16, 4096, 1536], P('exp', None, 'ctx'), may hold values from -0.09375 to 0.09375
- down_proj: bfloat16 [16, 1536, 4096], P('exp', 'ctx'), may hold values from -0.4375 to 0.4375
Outputs:
- mixed: bfloat16 [1024, 4096], P(('rep', 'ctx', 'exp')), parts along dimension 0
- expert_sum: bfloat16 [1024, 4096], P(('rep', 'ctx', 'exp')), parts along dimension 0
The draws below stay inside these ranges and needn't reach their ends.
There are 2 independent parts, one for each index of `rep`. The reference program is written for one: setup_inputs(seed, part) draws one part's arguments, and reference() takes and returns one part's arrays. A program takes and returns all parts, laid end to end along the dimension named above; an argument that names none is the same for every part. Nothing has to cross between parts.
Inputs may be any that keep to these rules, and one draw needn't show every extreme that they name: `expert_ids`: each row names 8 different experts; among the 32 rows of one device no expert is named by more than 2 rows. `live_counts`: some device has all of its rows live.
All inputs are finite; a program needn't handle non-finite values.
Results may differ from the reference program's by a relative error of at most 0.023.
Values may be sent and summed in bfloat16 or wider, within the bound.
A program may use at most 128 MiB of HBM per device.

```python
import math
import jax
import jax.numpy as jnp
import numpy as np
from jax import lax

D = 4096
HEADS = 64
KV_HEADS = 4
HEAD_DIM = 128
FF = 1536
EXPERTS = 128
TOPK = 8
CAP = 2
PASS_EXPERTS = 16
GROUPS = 16
ROWS = 32
LENGTH = 512
N_CTX = 1
N_EXP = 16


def attention_inputs(key):
    base = jax.random.fold_in(key, 7)
    first_key, second_key = jax.random.split(base, 2)
    keys_all = jnp.clip(jax.random.normal(first_key, (LENGTH, KV_HEADS, HEAD_DIM), jnp.float32), -6.0, 6.0)
    queries_all = jnp.clip(jax.random.normal(second_key, (LENGTH, HEADS, HEAD_DIM), jnp.float32), -6.0, 6.0)
    return (queries_all.reshape(LENGTH, HEADS * HEAD_DIM), keys_all.reshape(LENGTH, KV_HEADS * HEAD_DIM))


def draw_queries(key, part):
    return attention_inputs(key)[0].astype(jnp.bfloat16)


def draw_keys(key, part):
    return attention_inputs(key)[1].astype(jnp.bfloat16)


def draw_live_counts(key, part):
    counts = jax.random.randint(key, (GROUPS,), ROWS // 2, ROWS + 1, dtype=jnp.int32)
    forced = jax.random.randint(jax.random.fold_in(key, 3), (), 0, GROUPS, dtype=jnp.int32)
    return jnp.where(jnp.arange(GROUPS, dtype=jnp.int32) == forced, ROWS, counts).astype(jnp.int32)


def plant(array, own_key, least, top_value):
    spot = [jax.random.randint(jax.random.fold_in(own_key, axis), (), 0, length) for axis, length in enumerate(array.shape)]
    main_axis = array.shape.index(max(array.shape))
    neighbour = spot[:main_axis] + [(spot[main_axis] + 1) % array.shape[main_axis]] + spot[main_axis + 1:]
    return array.at[tuple(spot)].set(least).at[tuple(neighbour)].set(top_value)


def shard_levels(rng, dims, cuts, smallest, top_value):
    level = 1.0
    for dim, parts in cuts:
        draws = jax.random.uniform(jax.random.fold_in(jax.random.fold_in(rng, 6), dim), (parts,), jnp.float32, smallest / len(cuts), top_value / len(cuts))
        level = level * jnp.repeat(jnp.exp(draws), dims[dim] // parts).reshape((-1,) + (1,) * (len(dims) - 1 - dim))
    return level


def routed_block(own_key, own, number, rows, count, top, bound, slope):
    order = jax.random.permutation(own_key, count)
    heavy_load, usual = shares(count, rows * top, bound, slope, True), shares(count, rows * top, bound, slope, False)
    places = jnp.arange(count)

    def named(sizes, rotation):
        used = int((sizes > 0).sum())
        fixed = max(1, used // 4)
        moved = fixed + (places - fixed + rotation * (used - fixed)) % max(1, count - fixed)
        return jnp.zeros((count,), jnp.int32).at[order[jnp.where(places < fixed, places, moved)]].set(jnp.asarray(sizes, jnp.int32))

    sizes = jnp.where(number % 4 == 0, named(heavy_load, number // 4), named(usual, number - number // 4 - 1))
    mixed = jax.random.permutation(jax.random.fold_in(own, 3), count)
    source_of, sink = mixed[0:count // 2 * 2:2], mixed[1:count // 2 * 2:2]
    slack = jnp.minimum(sizes[source_of] - 1, bound - sizes[sink]) // 2
    slack = jnp.where((source_of == order[0]) | (sink == order[0]) | (sizes[sink] == 0), 0, jnp.maximum(slack, 0))
    moved = jax.random.randint(jax.random.fold_in(own, 4), (count // 2,), 0, 1 << 20) % (slack + 1)
    sizes = sizes.at[source_of].add(-moved).at[sink].add(moved)
    members = jnp.searchsorted(jnp.cumsum(sizes), jnp.arange(rows * top), side="right").astype(jnp.int32)
    listing = members.reshape(top, rows).T
    listing = listing[jax.random.permutation(jax.random.fold_in(own, 1), rows)]
    rotation = jax.random.randint(jax.random.fold_in(own, 2), (rows, 1), 0, top)
    return jnp.take_along_axis(listing, (jnp.arange(top)[None, :] + rotation) % top, axis=1)


def shares(number_of, total, limit, slope, full):
    portions = [(1 << 20) // math.isqrt(grade ** slope) + 1 for grade in range(1, number_of + 1)]
    largest = limit if full else min(limit, max(-(-total // number_of), total * portions[0] // sum(portions)))
    least = 1 if total - largest >= number_of - 1 else 0
    given, rest = [largest] + [least] * (number_of - 1), total - largest - least * (number_of - 1)
    while rest > 0:
        movable = [i for i in range(1, number_of) if given[i] < largest] or [i for i in range(1, number_of) if given[i] < limit]
        mass, budget = sum([portions[i] for i in movable]), rest
        for i in movable:
            addition = min(limit - given[i], max(1, budget * portions[i] // mass), rest)
            given[i] = given[i] + addition
            rest = rest - addition
    return np.array(given)


def normal_values(key, extent, deviation, bound, shards=(), kind=jnp.bfloat16):
    values = deviation * jax.random.normal(key, extent, jnp.float32)
    if shards:
        values = values * shard_levels(key, extent, shards, -0.22, 0.18)
    return jnp.clip(values, -bound, bound).astype(kind)


def setup_inputs(seed: int = 0, part: int = 0) -> dict:
    key_list = jax.random.split(jax.random.key(seed), 13)
    part_keys = jax.random.split(jax.random.fold_in(key_list[12], part), 13)
    hidden_in = normal_values(part_keys[0], (LENGTH, D), 1.0, 6.0, ((0, 16),))
    queries = draw_queries(jax.random.fold_in(jax.random.fold_in(key_list[12], part), 71), part)
    keys = draw_keys(jax.random.fold_in(jax.random.fold_in(key_list[12], part), 71), part)
    values = normal_values(part_keys[3], (LENGTH, KV_HEADS * HEAD_DIM), 1.0, 6.0)
    out_proj = normal_values(key_list[4], (HEADS * HEAD_DIM, D), (HEADS * HEAD_DIM) ** -0.5, 0.0625, ((0, 16),))
    norm_gain = jnp.clip(1.0 + 0.18 * jax.random.normal(key_list[5], (D,), jnp.float32), 0.1, 1.9)
    expert_ids_keys = jax.random.split(jax.random.fold_in(part_keys[6], 1), LENGTH // ROWS)
    expert_ids_turns = jax.random.permutation(jax.random.fold_in(part_keys[6], 3), LENGTH // ROWS)
    expert_ids = jax.vmap(lambda own, number: routed_block(jax.random.fold_in(part_keys[6], 2), own, number, ROWS, EXPERTS, TOPK, CAP, 2))(expert_ids_keys, expert_ids_turns).reshape((LENGTH, TOPK))
    gate_fixed = plant(jax.random.randint(part_keys[7], (LENGTH, TOPK), 1, 4097), jax.random.fold_in(part_keys[7], 1), 1, 4096).astype(jnp.int32)
    live_counts = draw_live_counts(jax.random.fold_in(jax.random.fold_in(key_list[12], part), 71), part)
    gate_proj = normal_values(key_list[9], (PASS_EXPERTS, D, FF), D ** -0.5, 0.09375, ((0, 16),))
    up_proj = normal_values(key_list[10], (PASS_EXPERTS, D, FF), D ** -0.5, 0.09375, ((0, 16),))
    down_proj = normal_values(key_list[11], (PASS_EXPERTS, FF, D), (FF // 8) ** -0.5, 0.4375, ((0, 16),))
    return {"hidden_in": hidden_in, "queries": queries, "keys": keys, "values": values, "out_proj": out_proj, "norm_gain": norm_gain, "expert_ids": expert_ids, "gate_fixed": gate_fixed, "live_counts": live_counts, "gate_proj": gate_proj, "up_proj": up_proj, "down_proj": down_proj}


def attend_head(head, queries3, keys3, values3, visible):
    group = HEADS // KV_HEADS
    query_rows = lax.dynamic_index_in_dim(queries3, head, 1, keepdims=False)
    key_rows = lax.dynamic_index_in_dim(keys3, head // group, 1, keepdims=False)
    value_rows = lax.dynamic_index_in_dim(values3, head // group, 1, keepdims=False)
    scores = jnp.dot(query_rows, key_rows.T, preferred_element_type=jnp.float32) * HEAD_DIM ** (-0.5)
    scores = jnp.where(visible, scores, -jnp.inf)
    largest = lax.optimization_barrier(jnp.max(scores, axis=1, keepdims=True))
    weights = jnp.where(visible, jnp.exp(scores - largest), 0.0)
    total = lax.optimization_barrier(jnp.sum(weights, axis=1, keepdims=True))
    summed = jnp.dot(weights.astype(jnp.bfloat16), value_rows, preferred_element_type=jnp.float32)
    return (summed / total).astype(jnp.bfloat16)

def run_expert(operands):
    rows, w_gate, w_up, w_down = operands
    width = FF // N_CTX
    total = jnp.zeros((rows.shape[0], D), jnp.float32)
    for slice_index in range(N_CTX):
        lower = slice_index * width
        gate_part = jnp.dot(rows, w_gate[:, lower:lower + width], preferred_element_type=jnp.float32)
        up_part = jnp.dot(rows, w_up[:, lower:lower + width], preferred_element_type=jnp.float32)
        hidden = (jax.nn.silu(gate_part) * up_part).astype(jnp.bfloat16)
        partial_value = jnp.dot(hidden, w_down[lower:lower + width, :], preferred_element_type=jnp.float32)
        rounded = lax.optimization_barrier(partial_value.astype(jnp.bfloat16))
        total = total + rounded.astype(jnp.float32)
    return total.astype(jnp.bfloat16)

def add_group(total, operands):
    columns, weight_rows = operands
    part = jnp.dot(columns, weight_rows, preferred_element_type=jnp.float32).astype(jnp.bfloat16)
    part = lax.optimization_barrier(part)
    return (total + part.astype(jnp.float32), None)

def reference(hidden_in, queries, keys, values, out_proj, norm_gain, expert_ids, gate_fixed, live_counts, gate_proj, up_proj, down_proj):
    queries3 = queries.reshape(LENGTH, HEADS, HEAD_DIM)
    keys3 = keys.reshape(LENGTH, KV_HEADS, HEAD_DIM)
    values3 = values.reshape(LENGTH, KV_HEADS, HEAD_DIM)
    positions = jnp.arange(LENGTH, dtype=jnp.int32)
    visible = positions[None, :] <= positions[:, None]
    heads_out = lax.map(lambda head: attend_head(head, queries3, keys3, values3, visible), jnp.arange(HEADS, dtype=jnp.int32))
    attended = heads_out.transpose(1, 0, 2).reshape(LENGTH, HEADS * HEAD_DIM)
    columns = HEADS * HEAD_DIM // N_EXP
    grouped = attended.reshape(LENGTH, N_EXP, columns).transpose(1, 0, 2)
    weight_groups = out_proj.reshape(N_EXP, columns, D)
    projected, _ = lax.scan(add_group, jnp.zeros((LENGTH, D), jnp.float32), (grouped, weight_groups))
    residual = hidden_in.astype(jnp.float32) + projected
    mixed = residual.astype(jnp.bfloat16)
    scale = lax.rsqrt(lax.optimization_barrier(jnp.mean(residual * residual, axis=1, keepdims=True)) + 1e-06)
    normed = (residual * scale * norm_gain).astype(jnp.bfloat16)
    slots = PASS_EXPERTS * CAP
    chosen = expert_ids.reshape(GROUPS, ROWS, TOPK)
    live = jnp.arange(ROWS, dtype=jnp.int32)[None, :] < live_counts[:, None]
    active = (chosen < PASS_EXPERTS) & live[:, :, None]
    onehot = ((chosen[..., None] == jnp.arange(PASS_EXPERTS, dtype=jnp.int32)) & active[..., None]).astype(jnp.int32)
    onehot = onehot.reshape(GROUPS, ROWS * TOPK, PASS_EXPERTS)
    earlier = jnp.cumsum(onehot, axis=1) - onehot
    rank = lax.optimization_barrier(jnp.sum(earlier * onehot, axis=2)).reshape(GROUPS, ROWS, TOPK)
    slot = jnp.where(active, chosen * CAP + rank, -1)
    pair_hit = slot[..., None] == jnp.arange(slots, dtype=jnp.int32)
    dispatch = jnp.any(pair_hit, axis=2).astype(jnp.float32)
    sent = jnp.einsum('brs,brd->bsd', dispatch, normed.reshape(GROUPS, ROWS, D).astype(jnp.float32)).astype(jnp.bfloat16)
    expert_in = sent.reshape(GROUPS, PASS_EXPERTS, CAP, D).transpose(1, 0, 2, 3).reshape(PASS_EXPERTS, GROUPS * CAP, D)
    expert_out = lax.map(run_expert, (expert_in, gate_proj, up_proj, down_proj))
    returned = expert_out.reshape(PASS_EXPERTS, GROUPS, CAP, D).transpose(1, 0, 2, 3).reshape(GROUPS, slots, D)
    weights = gate_fixed.reshape(GROUPS, ROWS, TOPK).astype(jnp.float32) / 4096.0
    combine = lax.optimization_barrier(jnp.sum(pair_hit.astype(jnp.float32) * weights[..., None], axis=2))
    expert_sum = jnp.einsum('brs,bsd->brd', combine, returned.astype(jnp.float32), precision=lax.Precision.HIGHEST)
    return (mixed, expert_sum.reshape(LENGTH, D).astype(jnp.bfloat16))
```

```python
import jax
import jax.numpy as jnp
from jax import lax
from jax.experimental import pallas as pl
from jax.experimental.pallas import tpu as pltpu
from jax.sharding import PartitionSpec as P

D = 4096
HEADS = 64
KV_HEADS = 4
HEAD_DIM = 128
TOPK = 8
CAP = 2


N_EXP = 16
ROWS = 32
SEQ = N_EXP * ROWS
HEAD_COLS = 512
FF = 1536
WIDE = 512
CHUNKS = D // WIDE
SLOTS = N_EXP * CAP
QBLOCK = 256


def fused_kernel(
    hidden_ref,
    q_ref,
    k_ref,
    v_ref,
    gain_ref,
    ids_ref,
    fixed_ref,
    live_ref,
    proj_hbm,
    gate_hbm,
    up_hbm,
    down_hbm,
    mixed_ref,
    sum_ref,
    proj,
    gate,
    up,
    down,
    attended,
    part,
    got1,
    got2,
    got3,
    resid,
    rows,
    hid,
    send_rows,
    got_rows,
    send_back,
    got_back,
    load_sem,
    send1,
    recv1,
    send2,
    recv2,
    send3,
    recv3,
    send4,
    recv4,
    send5,
    recv5,
):
    me = lax.axis_index("exp")
    x, y, z = me % 2, (me // 2) % 2, me // 4
    loads = [
        pltpu.make_async_copy(source, target, load_sem.at[i])
        for i, (source, target) in enumerate(
            [(proj_hbm, proj), (gate_hbm.at[0], gate), (up_hbm.at[0], up), (down_hbm.at[0], down)]
        )
    ]
    for load in loads:
        load.start()

    barrier = pltpu.get_barrier_semaphore()
    for step in range(1, N_EXP):
        pl.semaphore_signal(
            barrier,
            inc=1,
            device_id={"exp": (me + step) % N_EXP},
            device_id_type=pl.DeviceIdType.MESH,
        )

    kv = (me * (HEAD_COLS // HEAD_DIM)) // (HEADS // KV_HEADS)
    kv_cols = pl.ds(pl.multiple_of(kv * HEAD_DIM, HEAD_DIM), HEAD_DIM)
    scale = HEAD_DIM ** (-0.5)
    for block in range(SEQ // QBLOCK):
        first = block * QBLOCK
        keys_seen = first + QBLOCK
        q_pos = first + lax.broadcasted_iota(jnp.int32, (QBLOCK, keys_seen), 0)
        k_pos = lax.broadcasted_iota(jnp.int32, (QBLOCK, keys_seen), 1)
        visible = k_pos <= q_pos
        for head in range(HEAD_COLS // HEAD_DIM):
            cols = slice(head * HEAD_DIM, (head + 1) * HEAD_DIM)
            scores = (
                lax.dot_general(
                    q_ref[first : first + QBLOCK, cols],
                    k_ref[:keys_seen, kv_cols],
                    (((1,), (1,)), ((), ())),
                    preferred_element_type=jnp.float32,
                )
                * scale
            )
            scores = jnp.where(visible, scores, -1e30)
            largest = jnp.max(scores, axis=1, keepdims=True)
            weights = jnp.exp(scores - largest)
            total = jnp.sum(weights, axis=1, keepdims=True)
            summed = jnp.dot(
                weights.astype(jnp.bfloat16),
                v_ref[:keys_seen, kv_cols],
                preferred_element_type=jnp.float32,
            )
            attended[first : first + QBLOCK, cols] = (summed / total).astype(jnp.bfloat16)

    loads[0].wait()
    pl.semaphore_wait(barrier, N_EXP - 1)

    x_peer, y_peer = me + 1 - 2 * x, me + 2 - 4 * y

    def places(odd):
        return (y, x, y_peer, x_peer) if odd else (x, y, x_peer, y_peer)

    def copy1(chunk, odd):
        a, _, peer, _ = places(odd)
        return pltpu.make_async_remote_copy(
            src_ref=part.at[chunk, 1 - a],
            dst_ref=got1.at[chunk],
            send_sem=send1.at[chunk],
            recv_sem=recv1.at[chunk],
            device_id={"exp": peer},
            device_id_type=pl.DeviceIdType.MESH,
        )

    def copy2(chunk, odd):
        a, b, _, peer = places(odd)
        return pltpu.make_async_remote_copy(
            src_ref=part.at[chunk, a, 1 - b],
            dst_ref=got2.at[chunk],
            send_sem=send2.at[chunk],
            recv_sem=recv2.at[chunk],
            device_id={"exp": peer},
            device_id_type=pl.DeviceIdType.MESH,
        )

    def copy3(chunk, odd, step):
        a, b, _, _ = places(odd)
        other = (z + step) % 4
        return pltpu.make_async_remote_copy(
            src_ref=part.at[chunk, a, b, other],
            dst_ref=got3.at[chunk, step - 1],
            send_sem=send3.at[chunk, step - 1],
            recv_sem=recv3.at[chunk, step - 1],
            device_id={"exp": me + (other - z) * 4},
            device_id_type=pl.DeviceIdType.MESH,
        )

    def project(pair, _):
        for odd in (0, 1):
            chunk = pair * 2 + odd
            cols = pl.ds(pl.multiple_of(chunk * WIDE, WIDE), WIDE)
            for half in range(2):
                lines = SEQ // 2
                product = jnp.dot(
                    attended[half * lines : (half + 1) * lines, :],
                    proj[:, cols],
                    preferred_element_type=jnp.float32,
                ).astype(jnp.bfloat16)
                for local in range(N_EXP // 2):
                    owner = half * (N_EXP // 2) + local
                    ox, oy, oz = owner % 2, (owner // 2) % 2, owner // 4
                    a, b = (oy, ox) if odd else (ox, oy)
                    part[chunk, a, b, oz] = product[local * ROWS : (local + 1) * ROWS, :]
            copy1(chunk, odd).start()
        return 0

    lax.fori_loop(0, CHUNKS // 2, project, 0)

    def fold1(pair, _):
        for odd in (0, 1):
            chunk = pair * 2 + odd
            a = places(odd)[0]
            copy1(chunk, odd).wait_recv()
            for b in range(2):
                for c in range(4):
                    part[chunk, a, b, c] = part[chunk, a, b, c] + got1[chunk, b, c]
            copy2(chunk, odd).start()
        return 0

    lax.fori_loop(0, CHUNKS // 2, fold1, 0)

    def fold2(pair, _):
        for odd in (0, 1):
            chunk = pair * 2 + odd
            a, b, _, _ = places(odd)
            copy2(chunk, odd).wait_recv()
            for c in range(4):
                part[chunk, a, b, c] = part[chunk, a, b, c] + got2[chunk, c]
            for step in range(1, 4):
                copy3(chunk, odd, step).start()
        return 0

    lax.fori_loop(0, CHUNKS // 2, fold2, 0)

    slot = lax.broadcasted_iota(jnp.int32, (ROWS, SLOTS), 1)
    row = lax.broadcasted_iota(jnp.int32, (ROWS, SLOTS), 0)
    weight = jnp.zeros((ROWS, SLOTS), jnp.int32)
    named = jnp.zeros((ROWS, SLOTS), jnp.float32)
    for k in range(TOPK):
        same = (ids_ref[:, k : k + 1] == slot // CAP) & (row < live_ref[0])
        weight = weight + jnp.where(same, fixed_ref[:, k : k + 1], 0)
        named = named + jnp.where(same, 1.0, 0.0)
    before = lax.broadcasted_iota(jnp.int32, (ROWS, ROWS), 1) < lax.broadcasted_iota(
        jnp.int32, (ROWS, ROWS), 0
    )
    earlier = jnp.dot(
        jnp.where(before, 1.0, 0.0).astype(jnp.bfloat16),
        named.astype(jnp.bfloat16),
        preferred_element_type=jnp.float32,
    )
    taken = (named > 0.5) & (jnp.abs(earlier - (slot % CAP).astype(jnp.float32)) < 0.5)
    dispatch = jnp.where(taken, 1.0, 0.0).astype(jnp.bfloat16)
    weight = jnp.where(taken, weight, 0)
    coarse = (weight // 64) * 64
    combine_hi = (coarse.astype(jnp.float32) / 4096.0).astype(jnp.bfloat16)
    combine_lo = ((weight - coarse).astype(jnp.float32) / 4096.0).astype(jnp.bfloat16)

    lines = SLOTS * CHUNKS
    i = lax.broadcasted_iota(jnp.int32, (lines, lines), 0)
    j = lax.broadcasted_iota(jnp.int32, (lines, lines), 1)
    to_work = jnp.where((i % SLOTS) * CHUNKS + i // SLOTS == j, 1.0, 0.0).astype(jnp.bfloat16)
    to_travel = jnp.where((j % SLOTS) * CHUNKS + j // SLOTS == i, 1.0, 0.0).astype(jnp.bfloat16)

    def reorder(matrix, value):
        return jnp.dot(matrix, value, preferred_element_type=jnp.float32).astype(jnp.bfloat16)

    squares = jnp.zeros((ROWS, 1), jnp.float32)
    for chunk in range(CHUNKS):
        a, b, _, _ = places(chunk % 2)
        for step in range(1, 4):
            copy3(chunk, chunk % 2, step).wait_recv()
        cols = slice(chunk * WIDE, (chunk + 1) * WIDE)
        total = part[chunk, a, b, z].astype(jnp.float32)
        for step in range(3):
            total = total + got3[chunk, step].astype(jnp.float32)
        total = total + hidden_ref[:, cols].astype(jnp.float32)
        mixed_ref[:, cols] = total.astype(jnp.bfloat16)
        resid[chunk] = total
        squares = squares + jnp.sum(total * total, axis=1, keepdims=True)
    norm = lax.rsqrt(squares / D + 1e-06)
    for chunk in range(CHUNKS):
        cols = slice(chunk * WIDE, (chunk + 1) * WIDE)
        normed = (resid[chunk] * norm * gain_ref[:, cols]).astype(jnp.bfloat16)
        picked = lax.dot_general(
            dispatch, normed, (((0,), (0,)), ((), ())), preferred_element_type=jnp.float32
        )
        rows[chunk * SLOTS : (chunk + 1) * SLOTS, :] = picked.astype(jnp.bfloat16)
    ordered = reorder(to_travel, rows[...])
    per = CAP * CHUNKS
    for e in range(N_EXP):
        send_rows[e] = ordered[e * per : (e + 1) * per, :]

    def exchange(source, target, send_sem, recv_sem, step):
        other = (me + step) % N_EXP
        return pltpu.make_async_remote_copy(
            src_ref=source.at[other],
            dst_ref=target.at[me],
            send_sem=send_sem.at[step - 1],
            recv_sem=recv_sem.at[step - 1],
            device_id={"exp": other},
            device_id_type=pl.DeviceIdType.MESH,
        )

    there = [exchange(send_rows, got_rows, send4, recv4, step) for step in range(1, N_EXP)]
    for copy in there:
        copy.start()
    got_rows[me] = send_rows[me]
    for load in loads[1:]:
        load.wait()
    for copy in there:
        copy.wait_recv()

    rows[...] = reorder(to_work, got_rows[...].reshape(lines, WIDE))
    tokens = jnp.concatenate(
        [rows[chunk * SLOTS : (chunk + 1) * SLOTS, :] for chunk in range(CHUNKS)], axis=1
    )
    for block in range(FF // 256):
        cols = slice(block * 256, (block + 1) * 256)
        gate_part = jnp.dot(tokens, gate[:, cols], preferred_element_type=jnp.float32)
        up_part = jnp.dot(tokens, up[:, cols], preferred_element_type=jnp.float32)
        hid[:, cols] = (gate_part / (1.0 + jnp.exp(-gate_part)) * up_part).astype(jnp.bfloat16)
    for chunk in range(CHUNKS):
        cols = slice(chunk * WIDE, (chunk + 1) * WIDE)
        rows[chunk * SLOTS : (chunk + 1) * SLOTS, :] = jnp.dot(
            hid[...], down[:, cols], preferred_element_type=jnp.float32
        ).astype(jnp.bfloat16)
    ordered = reorder(to_travel, rows[...])
    for e in range(N_EXP):
        send_back[e] = ordered[e * per : (e + 1) * per, :]

    back = [exchange(send_back, got_back, send5, recv5, step) for step in range(1, N_EXP)]
    for copy in back:
        copy.start()
    got_back[me] = send_back[me]
    for copy in back:
        copy.wait_recv()
    rows[...] = reorder(to_work, got_back[...].reshape(lines, WIDE))
    for chunk in range(CHUNKS):
        cols = slice(chunk * WIDE, (chunk + 1) * WIDE)
        returned = rows[chunk * SLOTS : (chunk + 1) * SLOTS, :]
        sum_ref[:, cols] = (
            jnp.dot(combine_hi, returned, preferred_element_type=jnp.float32)
            + jnp.dot(combine_lo, returned, preferred_element_type=jnp.float32)
        ).astype(jnp.bfloat16)

    def finish(pair, _):
        for odd in (0, 1):
            chunk = pair * 2 + odd
            copy1(chunk, odd).wait_send()
            copy2(chunk, odd).wait_send()
            for step in range(1, 4):
                copy3(chunk, odd, step).wait_send()
        return 0

    lax.fori_loop(0, CHUNKS // 2, finish, 0)
    for copy in there + back:
        copy.wait_send()


def on_device_fused(
    hidden_in,
    queries,
    keys,
    values,
    out_proj,
    norm_gain,
    expert_ids,
    gate_fixed,
    live_counts,
    gate_proj,
    up_proj,
    down_proj,
):
    bf16 = jnp.bfloat16
    dma = pltpu.SemaphoreType.DMA
    vmem = pl.BlockSpec(memory_space=pltpu.VMEM)
    hbm = pl.BlockSpec(memory_space=pl.ANY)
    travelling = pltpu.VMEM((N_EXP, CAP * CHUNKS, WIDE), bf16)
    return pl.pallas_call(
        fused_kernel,
        out_shape=(jax.ShapeDtypeStruct((ROWS, D), bf16), jax.ShapeDtypeStruct((ROWS, D), bf16)),
        in_specs=[vmem] * 7 + [pl.BlockSpec(memory_space=pltpu.SMEM)] + [hbm] * 4,
        out_specs=(vmem, vmem),
        scratch_shapes=[
            pltpu.VMEM((HEAD_COLS, D), bf16),
            pltpu.VMEM((D, FF), bf16),
            pltpu.VMEM((D, FF), bf16),
            pltpu.VMEM((FF, D), bf16),
            pltpu.VMEM((SEQ, HEAD_COLS), bf16),
            pltpu.VMEM((CHUNKS, 2, 2, 4, ROWS, WIDE), bf16),
            pltpu.VMEM((CHUNKS, 2, 4, ROWS, WIDE), bf16),
            pltpu.VMEM((CHUNKS, 4, ROWS, WIDE), bf16),
            pltpu.VMEM((CHUNKS, 3, ROWS, WIDE), bf16),
            pltpu.VMEM((CHUNKS, ROWS, WIDE), jnp.float32),
            pltpu.VMEM((SLOTS * CHUNKS, WIDE), bf16),
            pltpu.VMEM((SLOTS, FF), bf16),
            travelling,
            travelling,
            travelling,
            travelling,
            dma((4,)),
            dma((CHUNKS,)),
            dma((CHUNKS,)),
            dma((CHUNKS,)),
            dma((CHUNKS,)),
            dma((CHUNKS, 3)),
            dma((CHUNKS, 3)),
            dma((N_EXP - 1,)),
            dma((N_EXP - 1,)),
            dma((N_EXP - 1,)),
            dma((N_EXP - 1,)),
        ],
        compiler_params=pltpu.CompilerParams(
            collective_id=0, has_side_effects=True, vmem_limit_bytes=60 * 2**20
        ),
        name="decoder_layer",
    )(
        hidden_in,
        queries,
        keys,
        values,
        norm_gain.reshape(1, D),
        expert_ids,
        gate_fixed,
        live_counts,
        out_proj,
        gate_proj,
        up_proj,
        down_proj,
    )


def on_device_general(
    hidden_in,
    queries,
    keys,
    values,
    out_proj,
    norm_gain,
    expert_ids,
    gate_fixed,
    live_counts,
    gate_proj,
    up_proj,
    down_proj,
):
    n_ctx = lax.axis_size("ctx")
    n_exp = lax.axis_size("exp")
    seq_rows = queries.shape[0]
    local_heads = queries.shape[1] // HEAD_DIM
    group = HEADS // KV_HEADS
    kv_index = lax.axis_index("exp") * local_heads // group
    key_head = lax.dynamic_slice_in_dim(keys, kv_index * HEAD_DIM, HEAD_DIM, 1)
    value_head = lax.dynamic_slice_in_dim(values, kv_index * HEAD_DIM, HEAD_DIM, 1)
    query_heads = queries.reshape(seq_rows, local_heads, HEAD_DIM).transpose(1, 0, 2)
    query_pos = lax.axis_index("ctx") * seq_rows + jnp.arange(seq_rows, dtype=jnp.int32)
    scale = HEAD_DIM ** (-0.5)

    def update(carry, key_block, value_block, first):
        running, total, accum = carry
        scores = (
            jnp.einsum("hqd,kd->hqk", query_heads, key_block, preferred_element_type=jnp.float32)
            * scale
        )
        key_pos = first + jnp.arange(seq_rows, dtype=jnp.int32)
        visible = (key_pos[None, :] <= query_pos[:, None])[None]
        scores = jnp.where(visible, scores, -1e30)
        newest = jnp.maximum(running, jnp.max(scores, axis=2))
        weights = jnp.where(visible, jnp.exp(scores - newest[..., None]), 0.0)
        factor = jnp.exp(running - newest)
        total = total * factor + jnp.sum(weights, axis=2)
        accum = accum * factor[..., None] + jnp.einsum(
            "hqk,kd->hqd",
            weights.astype(jnp.bfloat16),
            value_block,
            preferred_element_type=jnp.float32,
        )
        return (newest, total, accum)

    start_state = (
        jnp.full((local_heads, seq_rows), -1e30, jnp.float32),
        jnp.zeros((local_heads, seq_rows), jnp.float32),
        jnp.zeros((local_heads, seq_rows, HEAD_DIM), jnp.float32),
    )
    carry = start_state
    key_piece = lax.all_gather(key_head, "ctx", axis=0, tiled=True)
    value_piece = lax.all_gather(value_head, "ctx", axis=0, tiled=True)
    blocks = key_piece.shape[0] // seq_rows
    key_blocks = key_piece.reshape(blocks, seq_rows, HEAD_DIM)
    value_blocks = value_piece.reshape(blocks, seq_rows, HEAD_DIM)
    firsts = jnp.arange(blocks, dtype=jnp.int32) * seq_rows

    def step(state, inputs):
        key_block, value_block, first = inputs
        state = update(state, key_block, value_block, first)
        return (state, None)

    carry, _ = lax.scan(step, carry, (key_blocks, value_blocks, firsts))
    running, total, accum = carry
    attended = (
        (accum / total[..., None])
        .astype(jnp.bfloat16)
        .transpose(1, 0, 2)
        .reshape(seq_rows, local_heads * HEAD_DIM)
    )
    token_rows = hidden_in.shape[0]
    attn_out = lax.psum_scatter(
        jnp.dot(attended, out_proj, preferred_element_type=jnp.float32).astype(jnp.bfloat16),
        "exp",
        scatter_dimension=0,
        tiled=True,
    ).astype(jnp.float32)
    residual = hidden_in.astype(jnp.float32) + attn_out
    mixed = residual.astype(jnp.bfloat16)
    norm_scale = lax.rsqrt(jnp.mean(residual * residual, axis=1, keepdims=True) + 1e-06)
    normed = (residual * norm_scale * norm_gain).astype(jnp.bfloat16)
    slot_count = n_exp * CAP
    live = jnp.arange(token_rows, dtype=jnp.int32) < live_counts[0]
    active = (expert_ids < n_exp) & live[:, None]
    onehot = (
        (expert_ids[..., None] == jnp.arange(n_exp, dtype=jnp.int32)) & active[..., None]
    ).astype(jnp.int32)
    onehot = onehot.reshape(token_rows * TOPK, n_exp)
    earlier = jnp.cumsum(onehot, axis=0) - onehot
    rank = jnp.sum(earlier * onehot, axis=1).reshape(token_rows, TOPK)
    slot = jnp.where(active, expert_ids * CAP + rank, -1)
    pair_hit = slot[..., None] == jnp.arange(slot_count, dtype=jnp.int32)
    dispatch = jnp.any(pair_hit, axis=1).astype(jnp.bfloat16)
    send = jnp.einsum("rs,rd->sd", dispatch, normed, preferred_element_type=jnp.float32).astype(
        jnp.bfloat16
    )
    send = send.reshape(n_exp, CAP, D)
    route_weights = gate_fixed.astype(jnp.float32) / 4096.0
    combine = jnp.sum(pair_hit.astype(jnp.float32) * route_weights[..., None], axis=1)
    copies = jnp.broadcast_to(send[None], (n_ctx, n_exp, CAP, D)).reshape(n_ctx * n_exp, CAP, D)
    rows3 = lax.all_to_all(copies, ("ctx", "exp"), split_axis=0, concat_axis=0, tiled=True)
    flat_rows = rows3.reshape(-1, D)
    gate_part = jnp.dot(flat_rows, gate_proj[0], preferred_element_type=jnp.float32)
    up_part = jnp.dot(flat_rows, up_proj[0], preferred_element_type=jnp.float32)
    hidden = (jax.nn.silu(gate_part) * up_part).astype(jnp.bfloat16)
    partial_value = jnp.dot(hidden, down_proj[0], preferred_element_type=jnp.float32)
    partial_value = partial_value.reshape(rows3.shape[0], rows3.shape[1], D).astype(jnp.bfloat16)
    returned = lax.all_to_all(
        partial_value, ("ctx", "exp"), split_axis=0, concat_axis=0, tiled=True
    )
    expert_out = (
        returned.astype(jnp.float32).reshape(n_ctx, slot_count, D).sum(axis=0).astype(jnp.bfloat16)
    )
    expert_sum = jnp.dot(combine, expert_out.astype(jnp.float32), precision=lax.Precision.HIGHEST)
    return (mixed, expert_sum.astype(jnp.bfloat16))


def solution(mesh):
    in_specs = (
        P(("rep", "ctx", "exp"), None),
        P(("rep", "ctx"), "exp"),
        P(("rep", "ctx"), None),
        P(("rep", "ctx"), None),
        P("exp", None),
        P(),
        P(("rep", "ctx", "exp"), None),
        P(("rep", "ctx", "exp"), None),
        P(("rep", "ctx", "exp")),
        P("exp", None, "ctx"),
        P("exp", None, "ctx"),
        P("exp", "ctx", None),
    )
    out_specs = (P(("rep", "ctx", "exp"), None), P(("rep", "ctx", "exp"), None))
    sizes = mesh.shape
    fused = sizes["ctx"] == 1 and sizes["exp"] == N_EXP
    body = on_device_fused if fused else on_device_general
    return jax.shard_map(
        body, mesh=mesh, in_specs=in_specs, out_specs=out_specs, check_vma=False
    )
```

```python
import jax
import jax.numpy as jnp
from jax import lax
from jax.experimental import pallas as pl
from jax.experimental.pallas import tpu as pltpu
from jax.sharding import PartitionSpec as P

D = 4096
HEADS = 64
KV_HEADS = 4
HEAD_DIM = 128
TOPK = 8
CAP = 2


N_EXP = 16
ROWS = 32
SEQ = N_EXP * ROWS
HEAD_COLS = 512
FF = 1536
WIDE = 512
CHUNKS = D // WIDE
SLOTS = N_EXP * CAP
QBLOCK = 256
PIECES = 8
PAIR = 2 * WIDE
HALVES = 2


def fused_kernel(
    hidden_ref,
    q_ref,
    k_ref,
    v_ref,
    gain_ref,
    ids_ref,
    fixed_ref,
    live_ref,
    proj_hbm,
    gate_hbm,
    up_hbm,
    down_hbm,
    mixed_ref,
    sum_ref,
    proj,
    gate,
    up,
    down,
    attended,
    part,
    got1,
    got2,
    got3,
    gate_sum,
    up_sum,
    hid,
    send_rows,
    got_rows,
    send_back,
    got_back,
    send_norm,
    got_norm,
    load_sem,
    send1,
    recv1,
    send2,
    recv2,
    send3,
    recv3,
    send4,
    recv4,
    send5,
    recv5,
    send6,
    recv6,
):
    me = lax.axis_index("exp")
    x, y, z = me % 2, (me // 2) % 2, me // 4
    loads = [
        pltpu.make_async_copy(source, target, load_sem.at[i])
        for i, (source, target) in enumerate(
            [(proj_hbm, proj), (gate_hbm.at[0], gate), (up_hbm.at[0], up), (down_hbm.at[0], down)]
        )
    ]
    for load in loads:
        load.start()

    barrier = pltpu.get_barrier_semaphore()
    for step in range(1, N_EXP):
        pl.semaphore_signal(
            barrier,
            inc=1,
            device_id={"exp": (me + step) % N_EXP},
            device_id_type=pl.DeviceIdType.MESH,
        )

    kv = (me * (HEAD_COLS // HEAD_DIM)) // (HEADS // KV_HEADS)
    kv_cols = pl.ds(pl.multiple_of(kv * HEAD_DIM, HEAD_DIM), HEAD_DIM)
    scale = HEAD_DIM ** (-0.5)
    for block in range(SEQ // QBLOCK):
        first = block * QBLOCK
        keys_seen = first + QBLOCK
        q_pos = first + lax.broadcasted_iota(jnp.int32, (QBLOCK, keys_seen), 0)
        k_pos = lax.broadcasted_iota(jnp.int32, (QBLOCK, keys_seen), 1)
        visible = k_pos <= q_pos
        for head in range(HEAD_COLS // HEAD_DIM):
            cols = slice(head * HEAD_DIM, (head + 1) * HEAD_DIM)
            scores = (
                lax.dot_general(
                    q_ref[first : first + QBLOCK, cols],
                    k_ref[:keys_seen, kv_cols],
                    (((1,), (1,)), ((), ())),
                    preferred_element_type=jnp.float32,
                )
                * scale
            )
            scores = jnp.where(visible, scores, -1e30)
            largest = jnp.max(scores, axis=1, keepdims=True)
            weights = jnp.exp(scores - largest)
            total = jnp.sum(weights, axis=1, keepdims=True)
            summed = jnp.dot(
                weights.astype(jnp.bfloat16),
                v_ref[:keys_seen, kv_cols],
                preferred_element_type=jnp.float32,
            )
            attended[first : first + QBLOCK, cols] = (summed / total).astype(jnp.bfloat16)

    loads[0].wait()
    pl.semaphore_wait(barrier, N_EXP - 1)

    x_peer, y_peer = me + 1 - 2 * x, me + 2 - 4 * y

    def places(odd):
        return (y, x, y_peer, x_peer) if odd else (x, y, x_peer, y_peer)

    def copy1(chunk, odd):
        a, _, peer, _ = places(odd)
        return pltpu.make_async_remote_copy(
            src_ref=part.at[chunk, 1 - a],
            dst_ref=got1.at[chunk],
            send_sem=send1.at[chunk],
            recv_sem=recv1.at[chunk],
            device_id={"exp": peer},
            device_id_type=pl.DeviceIdType.MESH,
        )

    def copy2(chunk, odd):
        a, b, _, peer = places(odd)
        return pltpu.make_async_remote_copy(
            src_ref=part.at[chunk, a, 1 - b],
            dst_ref=got2.at[chunk],
            send_sem=send2.at[chunk],
            recv_sem=recv2.at[chunk],
            device_id={"exp": peer},
            device_id_type=pl.DeviceIdType.MESH,
        )

    def copy3(chunk, odd, step):
        a, b, _, _ = places(odd)
        other = (z + step) % 4
        return pltpu.make_async_remote_copy(
            src_ref=part.at[chunk, a, b, other],
            dst_ref=got3.at[chunk, step - 1],
            send_sem=send3.at[chunk, step - 1],
            recv_sem=recv3.at[chunk, step - 1],
            device_id={"exp": me + (other - z) * 4},
            device_id_type=pl.DeviceIdType.MESH,
        )

    def project(pair):
        for odd in (0, 1):
            chunk = pair * 2 + odd
            cols = slice(chunk * WIDE, (chunk + 1) * WIDE)
            for half in range(2):
                lines = SEQ // 2
                product = jnp.dot(
                    attended[half * lines : (half + 1) * lines, :],
                    proj[:, cols],
                    preferred_element_type=jnp.float32,
                ).astype(jnp.bfloat16)
                for local in range(N_EXP // 2):
                    owner = half * (N_EXP // 2) + local
                    ox, oy, oz = owner % 2, (owner // 2) % 2, owner // 4
                    a, b = (oy, ox) if odd else (ox, oy)
                    part[chunk, a, b, oz] = product[local * ROWS : (local + 1) * ROWS, :]
            copy1(chunk, odd).start()

    def fold1(pair):
        for odd in (0, 1):
            chunk = pair * 2 + odd
            a = places(odd)[0]
            copy1(chunk, odd).wait_recv()
            for b in range(2):
                for c in range(4):
                    part[chunk, a, b, c] = part[chunk, a, b, c] + got1[chunk, b, c]
            copy2(chunk, odd).start()

    def fold2(pair):
        for odd in (0, 1):
            chunk = pair * 2 + odd
            a, b, _, _ = places(odd)
            copy2(chunk, odd).wait_recv()
            for c in range(4):
                part[chunk, a, b, c] = part[chunk, a, b, c] + got2[chunk, c]
            for step in range(1, 4):
                copy3(chunk, odd, step).start()

    project(0)
    project(1)

    slot = lax.broadcasted_iota(jnp.int32, (SLOTS, ROWS), 0)
    row = lax.broadcasted_iota(jnp.int32, (SLOTS, ROWS), 1)
    weight = jnp.zeros((SLOTS, ROWS), jnp.int32)
    named = jnp.zeros((SLOTS, ROWS), jnp.float32)
    for k in range(TOPK):
        same = (ids_ref[k : k + 1, :] == slot // CAP) & (row < live_ref[0])
        weight = weight + jnp.where(same, fixed_ref[k : k + 1, :], 0)
        named = named + jnp.where(same, 1.0, 0.0)
    before = lax.broadcasted_iota(jnp.int32, (ROWS, ROWS), 0) < lax.broadcasted_iota(
        jnp.int32, (ROWS, ROWS), 1
    )
    earlier = jnp.dot(
        named.astype(jnp.bfloat16),
        jnp.where(before, 1.0, 0.0).astype(jnp.bfloat16),
        preferred_element_type=jnp.float32,
    )
    taken = (named > 0.5) & (jnp.abs(earlier - (slot % CAP).astype(jnp.float32)) < 0.5)
    dispatch_exact = jnp.where(taken, 1.0, 0.0)
    dispatch = dispatch_exact.astype(jnp.bfloat16)
    weight = jnp.where(taken, weight, 0)
    coarse = (weight // 64) * 64
    combine_hi = (coarse.astype(jnp.float32) / 4096.0).astype(jnp.bfloat16)
    combine_lo = ((weight - coarse).astype(jnp.float32) / 4096.0).astype(jnp.bfloat16)

    lines = SLOTS * PIECES
    per = CAP * PIECES
    i = lax.broadcasted_iota(jnp.int32, (lines, lines), 0)
    j = lax.broadcasted_iota(jnp.int32, (lines, lines), 1)
    to_work = jnp.where((i % SLOTS) * PIECES + i // SLOTS == j, 1.0, 0.0).astype(jnp.bfloat16)
    to_travel = jnp.where((j % SLOTS) * PIECES + j // SLOTS == i, 1.0, 0.0).astype(jnp.bfloat16)

    def reorder(matrix, value):
        return jnp.dot(matrix, value, preferred_element_type=jnp.float32).astype(jnp.bfloat16)

    def pieces_of(value):
        width = value.shape[1] // PIECES
        return jnp.concatenate(
            [value[:, p * width : (p + 1) * width] for p in range(PIECES)], axis=0
        )

    def whole_of(value):
        return jnp.concatenate(
            [value[p * SLOTS : (p + 1) * SLOTS, :] for p in range(PIECES)], axis=1
        )

    def exchange(source, target, send_sem, recv_sem, part_index, step):
        other = (me + step) % N_EXP
        return pltpu.make_async_remote_copy(
            src_ref=source.at[part_index, other],
            dst_ref=target.at[part_index, me],
            send_sem=send_sem.at[part_index, step - 1],
            recv_sem=recv_sem.at[part_index, step - 1],
            device_id={"exp": other},
            device_id_type=pl.DeviceIdType.MESH,
        )

    def there(pair, step):
        return exchange(send_rows, got_rows, send4, recv4, pair, step)

    def back(half, step):
        return exchange(send_back, got_back, send5, recv5, half, step)

    def norms(step):
        return exchange(send_norm, got_norm, send6, recv6, 0, step)

    def each_step(action):
        def body(step, _):
            action(step)
            return 0

        lax.fori_loop(1, N_EXP, body, 0)

    squares = [jnp.zeros((ROWS, 1), jnp.float32)]

    def final(pair):
        picked = []
        for odd in (0, 1):
            chunk = pair * 2 + odd
            a, b, _, _ = places(odd)
            for step in range(1, 4):
                copy3(chunk, odd, step).wait_recv()
            cols = slice(chunk * WIDE, (chunk + 1) * WIDE)
            total = part[chunk, a, b, z].astype(jnp.float32)
            for step in range(3):
                total = total + got3[chunk, step].astype(jnp.float32)
            total = total + hidden_ref[:, cols].astype(jnp.float32)
            mixed_ref[:, cols] = total.astype(jnp.bfloat16)
            squares[0] = squares[0] + jnp.sum(total * total, axis=1, keepdims=True)
            gained = (total * gain_ref[:, cols]).astype(jnp.bfloat16)
            picked.append(reorder(dispatch, gained))
        ordered = reorder(to_travel, pieces_of(jnp.concatenate(picked, axis=1)))
        for e in range(N_EXP):
            send_rows[pair, e] = ordered[e * per : (e + 1) * per, :]
        each_step(lambda step: there(pair, step).start())
        got_rows[pair, me] = send_rows[pair, me]

    def send_norms():
        norm = lax.rsqrt(squares[0] / D + 1e-06)
        wide = jnp.broadcast_to(norm, (ROWS, 128))
        slot_norm = jnp.dot(
            dispatch_exact, wide, precision=lax.Precision.HIGHEST, preferred_element_type=jnp.float32
        )
        line = lax.broadcasted_iota(jnp.int32, (N_EXP * 8, SLOTS), 0)
        source = lax.broadcasted_iota(jnp.int32, (N_EXP * 8, SLOTS), 1)
        spread = jnp.where((line // 8) * CAP + line % CAP == source, 1.0, 0.0)
        tiles = jnp.dot(
            spread, slot_norm, precision=lax.Precision.HIGHEST, preferred_element_type=jnp.float32
        )
        for e in range(N_EXP):
            send_norm[0, e] = tiles[e * 8 : (e + 1) * 8, :]
        each_step(lambda step: norms(step).start())
        got_norm[0, me] = send_norm[0, me]

    def receive_norms():
        each_step(lambda step: norms(step).wait_recv())
        line = lax.broadcasted_iota(jnp.int32, (SLOTS, N_EXP * 8), 1)
        target = lax.broadcasted_iota(jnp.int32, (SLOTS, N_EXP * 8), 0)
        gather = jnp.where((target // CAP) * 8 + target % CAP == line, 1.0, 0.0)
        return jnp.dot(
            gather,
            got_norm[0].reshape(N_EXP * 8, 128),
            precision=lax.Precision.HIGHEST,
            preferred_element_type=jnp.float32,
        )[:, :1]

    def expert_in(pair):
        if pair == 0:
            for load in loads[1:]:
                load.wait()
        each_step(lambda step: there(pair, step).wait_recv())
        tokens = whole_of(reorder(to_work, got_rows[pair].reshape(lines, PAIR // PIECES)))
        deep = slice(pair * PAIR, (pair + 1) * PAIR)
        for block in range(FF // 512):
            cols = slice(block * 512, (block + 1) * 512)
            for weights_in, sums in ((gate, gate_sum), (up, up_sum)):
                term = jnp.dot(tokens, weights_in[deep, cols], preferred_element_type=jnp.float32)
                sums[:, cols] = term if pair == 0 else sums[:, cols] + term

    fold1(0)
    project(2)
    fold1(1)
    fold2(0)
    project(3)
    fold1(2)
    fold2(1)
    final(0)
    fold1(3)
    fold2(2)
    final(1)
    expert_in(0)
    fold2(3)
    final(2)
    expert_in(1)
    final(3)
    send_norms()
    expert_in(2)
    expert_in(3)
    slot_scale = receive_norms()
    for block in range(FF // 512):
        cols = slice(block * 512, (block + 1) * 512)
        gate_part = gate_sum[:, cols] * slot_scale
        up_part = up_sum[:, cols] * slot_scale
        hid[:, cols] = (gate_part / (1.0 + jnp.exp(-gate_part)) * up_part).astype(jnp.bfloat16)

    width = D // HALVES
    for half in range(HALVES):
        partial_rows = []
        for block in range(width // WIDE):
            first = half * width + block * WIDE
            partial_rows.append(
                jnp.dot(
                    hid[...], down[:, first : first + WIDE], preferred_element_type=jnp.float32
                ).astype(jnp.bfloat16)
            )
        ordered = reorder(to_travel, pieces_of(jnp.concatenate(partial_rows, axis=1)))
        for e in range(N_EXP):
            send_back[half, e] = ordered[e * per : (e + 1) * per, :]
        for step in range(1, N_EXP):
            back(half, step).start()
        got_back[half, me] = send_back[half, me]
    for half in range(HALVES):
        each_step(lambda step: back(half, step).wait_recv())
        returned = whole_of(reorder(to_work, got_back[half].reshape(lines, width // PIECES)))
        over = (((0,), (0,)), ((), ()))
        sum_ref[:, half * width : (half + 1) * width] = (
            lax.dot_general(combine_hi, returned, over, preferred_element_type=jnp.float32)
            + lax.dot_general(combine_lo, returned, over, preferred_element_type=jnp.float32)
        ).astype(jnp.bfloat16)

    def finish(pair, _):
        for odd in (0, 1):
            chunk = pair * 2 + odd
            copy1(chunk, odd).wait_send()
            copy2(chunk, odd).wait_send()
            for step in range(1, 4):
                copy3(chunk, odd, step).wait_send()
        each_step(lambda step: there(pair, step).wait_send())
        return 0

    lax.fori_loop(0, CHUNKS // 2, finish, 0)
    each_step(lambda step: norms(step).wait_send())
    for half in range(HALVES):
        each_step(lambda step: back(half, step).wait_send())


def on_device_fused(
    hidden_in,
    queries,
    keys,
    values,
    out_proj,
    norm_gain,
    expert_ids,
    gate_fixed,
    live_counts,
    gate_proj,
    up_proj,
    down_proj,
):
    bf16 = jnp.bfloat16
    dma = pltpu.SemaphoreType.DMA
    vmem = pl.BlockSpec(memory_space=pltpu.VMEM)
    hbm = pl.BlockSpec(memory_space=pl.ANY)
    going = pltpu.VMEM((D // PAIR, N_EXP, CAP * PIECES, PAIR // PIECES), bf16)
    coming = pltpu.VMEM((HALVES, N_EXP, CAP * PIECES, D // HALVES // PIECES), bf16)
    norm_tiles = pltpu.VMEM((1, N_EXP, 8, 128), jnp.float32)
    return pl.pallas_call(
        fused_kernel,
        out_shape=(jax.ShapeDtypeStruct((ROWS, D), bf16), jax.ShapeDtypeStruct((ROWS, D), bf16)),
        in_specs=[vmem] * 7 + [pl.BlockSpec(memory_space=pltpu.SMEM)] + [hbm] * 4,
        out_specs=(vmem, vmem),
        scratch_shapes=[
            pltpu.VMEM((HEAD_COLS, D), bf16),
            pltpu.VMEM((D, FF), bf16),
            pltpu.VMEM((D, FF), bf16),
            pltpu.VMEM((FF, D), bf16),
            pltpu.VMEM((SEQ, HEAD_COLS), bf16),
            pltpu.VMEM((CHUNKS, 2, 2, 4, ROWS, WIDE), bf16),
            pltpu.VMEM((CHUNKS, 2, 4, ROWS, WIDE), bf16),
            pltpu.VMEM((CHUNKS, 4, ROWS, WIDE), bf16),
            pltpu.VMEM((CHUNKS, 3, ROWS, WIDE), bf16),
            pltpu.VMEM((SLOTS, FF), jnp.float32),
            pltpu.VMEM((SLOTS, FF), jnp.float32),
            pltpu.VMEM((SLOTS, FF), bf16),
            going,
            going,
            coming,
            coming,
            norm_tiles,
            norm_tiles,
            dma((4,)),
            dma((CHUNKS,)),
            dma((CHUNKS,)),
            dma((CHUNKS,)),
            dma((CHUNKS,)),
            dma((CHUNKS, 3)),
            dma((CHUNKS, 3)),
            dma((D // PAIR, N_EXP - 1)),
            dma((D // PAIR, N_EXP - 1)),
            dma((HALVES, N_EXP - 1)),
            dma((HALVES, N_EXP - 1)),
            dma((1, N_EXP - 1)),
            dma((1, N_EXP - 1)),
        ],
        compiler_params=pltpu.CompilerParams(
            collective_id=0, has_side_effects=True, vmem_limit_bytes=56 * 2**20
        ),
        name="decoder_layer",
    )(
        hidden_in,
        queries,
        keys,
        values,
        norm_gain.reshape(1, D),
        expert_ids.T,
        gate_fixed.T,
        live_counts,
        out_proj,
        gate_proj,
        up_proj,
        down_proj,
    )


def on_device_general(
    hidden_in,
    queries,
    keys,
    values,
    out_proj,
    norm_gain,
    expert_ids,
    gate_fixed,
    live_counts,
    gate_proj,
    up_proj,
    down_proj,
):
    n_ctx = lax.axis_size("ctx")
    n_exp = lax.axis_size("exp")
    seq_rows = queries.shape[0]
    local_heads = queries.shape[1] // HEAD_DIM
    group = HEADS // KV_HEADS
    kv_index = lax.axis_index("exp") * local_heads // group
    key_head = lax.dynamic_slice_in_dim(keys, kv_index * HEAD_DIM, HEAD_DIM, 1)
    value_head = lax.dynamic_slice_in_dim(values, kv_index * HEAD_DIM, HEAD_DIM, 1)
    query_heads = queries.reshape(seq_rows, local_heads, HEAD_DIM).transpose(1, 0, 2)
    query_pos = lax.axis_index("ctx") * seq_rows + jnp.arange(seq_rows, dtype=jnp.int32)
    scale = HEAD_DIM ** (-0.5)

    def update(carry, key_block, value_block, first):
        running, total, accum = carry
        scores = (
            jnp.einsum("hqd,kd->hqk", query_heads, key_block, preferred_element_type=jnp.float32)
            * scale
        )
        key_pos = first + jnp.arange(seq_rows, dtype=jnp.int32)
        visible = (key_pos[None, :] <= query_pos[:, None])[None]
        scores = jnp.where(visible, scores, -1e30)
        newest = jnp.maximum(running, jnp.max(scores, axis=2))
        weights = jnp.where(visible, jnp.exp(scores - newest[..., None]), 0.0)
        factor = jnp.exp(running - newest)
        total = total * factor + jnp.sum(weights, axis=2)
        accum = accum * factor[..., None] + jnp.einsum(
            "hqk,kd->hqd",
            weights.astype(jnp.bfloat16),
            value_block,
            preferred_element_type=jnp.float32,
        )
        return (newest, total, accum)

    start_state = (
        jnp.full((local_heads, seq_rows), -1e30, jnp.float32),
        jnp.zeros((local_heads, seq_rows), jnp.float32),
        jnp.zeros((local_heads, seq_rows, HEAD_DIM), jnp.float32),
    )
    carry = start_state
    key_piece = lax.all_gather(key_head, "ctx", axis=0, tiled=True)
    value_piece = lax.all_gather(value_head, "ctx", axis=0, tiled=True)
    blocks = key_piece.shape[0] // seq_rows
    key_blocks = key_piece.reshape(blocks, seq_rows, HEAD_DIM)
    value_blocks = value_piece.reshape(blocks, seq_rows, HEAD_DIM)
    firsts = jnp.arange(blocks, dtype=jnp.int32) * seq_rows

    def step(state, inputs):
        key_block, value_block, first = inputs
        state = update(state, key_block, value_block, first)
        return (state, None)

    carry, _ = lax.scan(step, carry, (key_blocks, value_blocks, firsts))
    running, total, accum = carry
    attended = (
        (accum / total[..., None])
        .astype(jnp.bfloat16)
        .transpose(1, 0, 2)
        .reshape(seq_rows, local_heads * HEAD_DIM)
    )
    token_rows = hidden_in.shape[0]
    attn_out = lax.psum_scatter(
        jnp.dot(attended, out_proj, preferred_element_type=jnp.float32).astype(jnp.bfloat16),
        "exp",
        scatter_dimension=0,
        tiled=True,
    ).astype(jnp.float32)
    residual = hidden_in.astype(jnp.float32) + attn_out
    mixed = residual.astype(jnp.bfloat16)
    norm_scale = lax.rsqrt(jnp.mean(residual * residual, axis=1, keepdims=True) + 1e-06)
    normed = (residual * norm_scale * norm_gain).astype(jnp.bfloat16)
    slot_count = n_exp * CAP
    live = jnp.arange(token_rows, dtype=jnp.int32) < live_counts[0]
    active = (expert_ids < n_exp) & live[:, None]
    onehot = (
        (expert_ids[..., None] == jnp.arange(n_exp, dtype=jnp.int32)) & active[..., None]
    ).astype(jnp.int32)
    onehot = onehot.reshape(token_rows * TOPK, n_exp)
    earlier = jnp.cumsum(onehot, axis=0) - onehot
    rank = jnp.sum(earlier * onehot, axis=1).reshape(token_rows, TOPK)
    slot = jnp.where(active, expert_ids * CAP + rank, -1)
    pair_hit = slot[..., None] == jnp.arange(slot_count, dtype=jnp.int32)
    dispatch = jnp.any(pair_hit, axis=1).astype(jnp.bfloat16)
    send = jnp.einsum("rs,rd->sd", dispatch, normed, preferred_element_type=jnp.float32).astype(
        jnp.bfloat16
    )
    send = send.reshape(n_exp, CAP, D)
    route_weights = gate_fixed.astype(jnp.float32) / 4096.0
    combine = jnp.sum(pair_hit.astype(jnp.float32) * route_weights[..., None], axis=1)
    copies = jnp.broadcast_to(send[None], (n_ctx, n_exp, CAP, D)).reshape(n_ctx * n_exp, CAP, D)
    rows3 = lax.all_to_all(copies, ("ctx", "exp"), split_axis=0, concat_axis=0, tiled=True)
    flat_rows = rows3.reshape(-1, D)
    gate_part = jnp.dot(flat_rows, gate_proj[0], preferred_element_type=jnp.float32)
    up_part = jnp.dot(flat_rows, up_proj[0], preferred_element_type=jnp.float32)
    hidden = (jax.nn.silu(gate_part) * up_part).astype(jnp.bfloat16)
    partial_value = jnp.dot(hidden, down_proj[0], preferred_element_type=jnp.float32)
    partial_value = partial_value.reshape(rows3.shape[0], rows3.shape[1], D).astype(jnp.bfloat16)
    returned = lax.all_to_all(
        partial_value, ("ctx", "exp"), split_axis=0, concat_axis=0, tiled=True
    )
    expert_out = (
        returned.astype(jnp.float32).reshape(n_ctx, slot_count, D).sum(axis=0).astype(jnp.bfloat16)
    )
    expert_sum = jnp.dot(combine, expert_out.astype(jnp.float32), precision=lax.Precision.HIGHEST)
    return (mixed, expert_sum.astype(jnp.bfloat16))


def solution(mesh):
    in_specs = (
        P(("rep", "ctx", "exp"), None),
        P(("rep", "ctx"), "exp"),
        P(("rep", "ctx"), None),
        P(("rep", "ctx"), None),
        P("exp", None),
        P(),
        P(("rep", "ctx", "exp"), None),
        P(("rep", "ctx", "exp"), None),
        P(("rep", "ctx", "exp")),
        P("exp", None, "ctx"),
        P("exp", None, "ctx"),
        P("exp", "ctx", None),
    )
    out_specs = (P(("rep", "ctx", "exp"), None), P(("rep", "ctx", "exp"), None))
    sizes = mesh.shape
    fused = sizes["ctx"] == 1 and sizes["exp"] == N_EXP
    body = on_device_fused if fused else on_device_general
    return jax.shard_map(
        body, mesh=mesh, in_specs=in_specs, out_specs=out_specs, check_vma=False
    )
```

```python
import jax
import jax.numpy as jnp
from jax import lax
from jax.experimental import pallas as pl
from jax.experimental.pallas import tpu as pltpu
from jax.sharding import PartitionSpec as P

D = 4096
HEADS = 64
KV_HEADS = 4
HEAD_DIM = 128
TOPK = 8
CAP = 2


N_EXP = 16
ROWS = 32
SEQ = N_EXP * ROWS
HEAD_COLS = 512
FF = 1536
WIDE = 512
CHUNKS = D // WIDE
SLOTS = N_EXP * CAP
QBLOCK = 256
PIECES = 8
PAIR = 2 * WIDE
HALVES = 2


def fused_kernel(
    hidden_ref,
    q_ref,
    k_ref,
    v_ref,
    gain_ref,
    ids_ref,
    fixed_ref,
    live_ref,
    proj_hbm,
    gate_hbm,
    up_hbm,
    down_hbm,
    mixed_ref,
    sum_ref,
    proj,
    gate,
    up,
    down,
    attended,
    part,
    got1,
    got2,
    got3,
    gate_sum,
    up_sum,
    hid,
    send_rows,
    got_rows,
    send_back,
    got_back,
    send_norm,
    got_norm,
    load_sem,
    send1,
    recv1,
    send2,
    recv2,
    send3,
    recv3,
    send4,
    recv4,
    send5,
    recv5,
    send6,
    recv6,
):
    me = lax.axis_index("exp")
    x, y, z = me % 2, (me // 2) % 2, me // 4
    loads = [
        pltpu.make_async_copy(source, target, load_sem.at[i])
        for i, (source, target) in enumerate(
            [(proj_hbm, proj), (gate_hbm.at[0], gate), (up_hbm.at[0], up), (down_hbm.at[0], down)]
        )
    ]
    for load in loads:
        load.start()

    barrier = pltpu.get_barrier_semaphore()
    for step in range(1, N_EXP):
        pl.semaphore_signal(
            barrier,
            inc=1,
            device_id={"exp": (me + step) % N_EXP},
            device_id_type=pl.DeviceIdType.MESH,
        )

    kv = (me * (HEAD_COLS // HEAD_DIM)) // (HEADS // KV_HEADS)
    kv_cols = pl.ds(pl.multiple_of(kv * HEAD_DIM, HEAD_DIM), HEAD_DIM)
    scale = HEAD_DIM ** (-0.5)

    def attend(block):
        first = block * QBLOCK
        keys_seen = first + QBLOCK
        q_pos = first + lax.broadcasted_iota(jnp.int32, (QBLOCK, keys_seen), 0)
        k_pos = lax.broadcasted_iota(jnp.int32, (QBLOCK, keys_seen), 1)
        visible = k_pos <= q_pos
        for head in range(HEAD_COLS // HEAD_DIM):
            cols = slice(head * HEAD_DIM, (head + 1) * HEAD_DIM)
            scores = (
                lax.dot_general(
                    q_ref[first : first + QBLOCK, cols],
                    k_ref[:keys_seen, kv_cols],
                    (((1,), (1,)), ((), ())),
                    preferred_element_type=jnp.float32,
                )
                * scale
            )
            scores = jnp.where(visible, scores, -1e30)
            largest = jnp.max(scores, axis=1, keepdims=True)
            weights = jnp.exp(scores - largest)
            total = jnp.sum(weights, axis=1, keepdims=True)
            summed = jnp.dot(
                weights.astype(jnp.bfloat16),
                v_ref[:keys_seen, kv_cols],
                preferred_element_type=jnp.float32,
            )
            attended[first : first + QBLOCK, cols] = (summed / total).astype(jnp.bfloat16)

    x_peer, y_peer = me + 1 - 2 * x, me + 2 - 4 * y

    def places(odd):
        return (y, x, y_peer, x_peer) if odd else (x, y, x_peer, y_peer)

    def copy1(chunk, odd, half):
        a, _, peer, _ = places(odd)
        return pltpu.make_async_remote_copy(
            src_ref=part.at[chunk, 1 - a, half],
            dst_ref=got1.at[chunk, half],
            send_sem=send1.at[chunk, half],
            recv_sem=recv1.at[chunk, half],
            device_id={"exp": peer},
            device_id_type=pl.DeviceIdType.MESH,
        )

    def copy2(chunk, odd, half):
        a, b, _, peer = places(odd)
        return pltpu.make_async_remote_copy(
            src_ref=part.at[chunk, a, half, 1 - b],
            dst_ref=got2.at[chunk, half],
            send_sem=send2.at[chunk, half],
            recv_sem=recv2.at[chunk, half],
            device_id={"exp": peer},
            device_id_type=pl.DeviceIdType.MESH,
        )

    def copy3(chunk, odd, step):
        a, b, _, _ = places(odd)
        other = (z + step) % 4
        return pltpu.make_async_remote_copy(
            src_ref=part.at[chunk, a, other // 2, b, other % 2],
            dst_ref=got3.at[chunk, step - 1],
            send_sem=send3.at[chunk, step - 1],
            recv_sem=recv3.at[chunk, step - 1],
            device_id={"exp": me + (other - z) * 4},
            device_id_type=pl.DeviceIdType.MESH,
        )

    def project(pair, half):
        lines = SEQ // 2
        for odd in (0, 1):
            chunk = pair * 2 + odd
            cols = slice(chunk * WIDE, (chunk + 1) * WIDE)
            product = jnp.dot(
                attended[half * lines : (half + 1) * lines, :],
                proj[:, cols],
                preferred_element_type=jnp.float32,
            ).astype(jnp.bfloat16)
            for local in range(N_EXP // 2):
                ox, oy, oz = local % 2, (local // 2) % 2, local // 4
                a, b = (oy, ox) if odd else (ox, oy)
                part[chunk, a, half, b, oz] = product[local * ROWS : (local + 1) * ROWS, :]
            copy1(chunk, odd, half).start()

    def fold1(pair, half):
        for odd in (0, 1):
            chunk = pair * 2 + odd
            a, b, _, _ = places(odd)
            copy1(chunk, odd, half).wait_recv()
            for c in range(2):
                part[chunk, a, half, 1 - b, c] = (
                    part[chunk, a, half, 1 - b, c] + got1[chunk, half, 1 - b, c]
                )
            copy2(chunk, odd, half).start()
            for c in range(2):
                part[chunk, a, half, b, c] = part[chunk, a, half, b, c] + got1[chunk, half, b, c]

    def fold2(pair):
        for odd in (0, 1):
            chunk = pair * 2 + odd
            a, b, _, _ = places(odd)
            for half in range(2):
                copy2(chunk, odd, half).wait_recv()
                for c in range(2):
                    part[chunk, a, half, b, c] = part[chunk, a, half, b, c] + got2[chunk, half, c]
            for step in range(1, 4):
                copy3(chunk, odd, step).start()

    attend(0)
    loads[0].wait()
    pl.semaphore_wait(barrier, N_EXP - 1)
    for pair in range(CHUNKS // 2):
        project(pair, 0)
    attend(1)
    project(0, 1)
    project(1, 1)

    slot = lax.broadcasted_iota(jnp.int32, (SLOTS, ROWS), 0)
    row = lax.broadcasted_iota(jnp.int32, (SLOTS, ROWS), 1)
    weight = jnp.zeros((SLOTS, ROWS), jnp.int32)
    named = jnp.zeros((SLOTS, ROWS), jnp.float32)
    for k in range(TOPK):
        same = (ids_ref[k : k + 1, :] == slot // CAP) & (row < live_ref[0])
        weight = weight + jnp.where(same, fixed_ref[k : k + 1, :], 0)
        named = named + jnp.where(same, 1.0, 0.0)
    before = lax.broadcasted_iota(jnp.int32, (ROWS, ROWS), 0) < lax.broadcasted_iota(
        jnp.int32, (ROWS, ROWS), 1
    )
    earlier = jnp.dot(
        named.astype(jnp.bfloat16),
        jnp.where(before, 1.0, 0.0).astype(jnp.bfloat16),
        preferred_element_type=jnp.float32,
    )
    taken = (named > 0.5) & (jnp.abs(earlier - (slot % CAP).astype(jnp.float32)) < 0.5)
    dispatch_exact = jnp.where(taken, 1.0, 0.0)
    dispatch = dispatch_exact.astype(jnp.bfloat16)
    weight = jnp.where(taken, weight, 0)
    coarse = (weight // 64) * 64
    combine_hi = (coarse.astype(jnp.float32) / 4096.0).astype(jnp.bfloat16)
    combine_lo = ((weight - coarse).astype(jnp.float32) / 4096.0).astype(jnp.bfloat16)

    lines = SLOTS * PIECES
    per = CAP * PIECES
    i = lax.broadcasted_iota(jnp.int32, (lines, lines), 0)
    j = lax.broadcasted_iota(jnp.int32, (lines, lines), 1)
    to_work = jnp.where((i % SLOTS) * PIECES + i // SLOTS == j, 1.0, 0.0).astype(jnp.bfloat16)
    to_travel = jnp.where((j % SLOTS) * PIECES + j // SLOTS == i, 1.0, 0.0).astype(jnp.bfloat16)

    def reorder(matrix, value):
        return jnp.dot(matrix, value, preferred_element_type=jnp.float32).astype(jnp.bfloat16)

    def pieces_of(value):
        width = value.shape[1] // PIECES
        return jnp.concatenate(
            [value[:, p * width : (p + 1) * width] for p in range(PIECES)], axis=0
        )

    def whole_of(value):
        return jnp.concatenate(
            [value[p * SLOTS : (p + 1) * SLOTS, :] for p in range(PIECES)], axis=1
        )

    def exchange(source, target, send_sem, recv_sem, part_index, step):
        other = (me + step) % N_EXP
        return pltpu.make_async_remote_copy(
            src_ref=source.at[part_index, other],
            dst_ref=target.at[part_index, me],
            send_sem=send_sem.at[part_index, step - 1],
            recv_sem=recv_sem.at[part_index, step - 1],
            device_id={"exp": other},
            device_id_type=pl.DeviceIdType.MESH,
        )

    def there(pair, step):
        return exchange(send_rows, got_rows, send4, recv4, pair, step)

    def back(half, step):
        return exchange(send_back, got_back, send5, recv5, half, step)

    def norms(step):
        return exchange(send_norm, got_norm, send6, recv6, 0, step)

    def each_step(action):
        def body(step, _):
            action(step)
            return 0

        lax.fori_loop(1, N_EXP, body, 0)

    squares = [jnp.zeros((ROWS, 1), jnp.float32)]

    def final(pair):
        picked = []
        for odd in (0, 1):
            chunk = pair * 2 + odd
            a, b, _, _ = places(odd)
            for step in range(1, 4):
                copy3(chunk, odd, step).wait_recv()
            cols = slice(chunk * WIDE, (chunk + 1) * WIDE)
            total = part[chunk, a, z // 2, b, z % 2].astype(jnp.float32)
            for step in range(3):
                total = total + got3[chunk, step].astype(jnp.float32)
            total = total + hidden_ref[:, cols].astype(jnp.float32)
            mixed_ref[:, cols] = total.astype(jnp.bfloat16)
            squares[0] = squares[0] + jnp.sum(total * total, axis=1, keepdims=True)
            gained = (total * gain_ref[:, cols]).astype(jnp.bfloat16)
            picked.append(reorder(dispatch, gained))
        ordered = reorder(to_travel, pieces_of(jnp.concatenate(picked, axis=1)))
        for e in range(N_EXP):
            send_rows[pair, e] = ordered[e * per : (e + 1) * per, :]
        each_step(lambda step: there(pair, step).start())
        got_rows[pair, me] = send_rows[pair, me]

    def send_norms():
        norm = lax.rsqrt(squares[0] / D + 1e-06)
        wide = jnp.broadcast_to(norm, (ROWS, 128))
        slot_norm = jnp.dot(
            dispatch_exact, wide, precision=lax.Precision.HIGHEST, preferred_element_type=jnp.float32
        )
        line = lax.broadcasted_iota(jnp.int32, (N_EXP * 8, SLOTS), 0)
        source = lax.broadcasted_iota(jnp.int32, (N_EXP * 8, SLOTS), 1)
        spread = jnp.where((line // 8) * CAP + line % CAP == source, 1.0, 0.0)
        tiles = jnp.dot(
            spread, slot_norm, precision=lax.Precision.HIGHEST, preferred_element_type=jnp.float32
        )
        for e in range(N_EXP):
            send_norm[0, e] = tiles[e * 8 : (e + 1) * 8, :]
        each_step(lambda step: norms(step).start())
        got_norm[0, me] = send_norm[0, me]

    def receive_norms():
        each_step(lambda step: norms(step).wait_recv())
        line = lax.broadcasted_iota(jnp.int32, (SLOTS, N_EXP * 8), 1)
        target = lax.broadcasted_iota(jnp.int32, (SLOTS, N_EXP * 8), 0)
        gather = jnp.where((target // CAP) * 8 + target % CAP == line, 1.0, 0.0)
        return jnp.dot(
            gather,
            got_norm[0].reshape(N_EXP * 8, 128),
            precision=lax.Precision.HIGHEST,
            preferred_element_type=jnp.float32,
        )[:, :1]

    def expert_in(pair):
        if pair == 0:
            for load in loads[1:]:
                load.wait()
        each_step(lambda step: there(pair, step).wait_recv())
        tokens = whole_of(reorder(to_work, got_rows[pair].reshape(lines, PAIR // PIECES)))
        deep = slice(pair * PAIR, (pair + 1) * PAIR)
        for block in range(FF // 512):
            cols = slice(block * 512, (block + 1) * 512)
            for weights_in, sums in ((gate, gate_sum), (up, up_sum)):
                term = jnp.dot(tokens, weights_in[deep, cols], preferred_element_type=jnp.float32)
                sums[:, cols] = term if pair == 0 else sums[:, cols] + term

    fold1(0, 0)
    fold1(1, 0)
    project(2, 1)
    fold1(0, 1)
    fold1(2, 0)
    project(3, 1)
    fold2(0)
    fold1(1, 1)
    fold1(3, 0)
    fold2(1)
    final(0)
    fold1(2, 1)
    fold2(2)
    final(1)
    fold1(3, 1)
    expert_in(0)
    fold2(3)
    final(2)
    expert_in(1)
    final(3)
    send_norms()
    expert_in(2)
    expert_in(3)
    slot_scale = receive_norms()
    for block in range(FF // 512):
        cols = slice(block * 512, (block + 1) * 512)
        gate_part = gate_sum[:, cols] * slot_scale
        up_part = up_sum[:, cols] * slot_scale
        hid[:, cols] = (gate_part / (1.0 + jnp.exp(-gate_part)) * up_part).astype(jnp.bfloat16)

    width = D // HALVES
    for half in range(HALVES):
        partial_rows = []
        for block in range(width // WIDE):
            first = half * width + block * WIDE
            partial_rows.append(
                jnp.dot(
                    hid[...], down[:, first : first + WIDE], preferred_element_type=jnp.float32
                ).astype(jnp.bfloat16)
            )
        ordered = reorder(to_travel, pieces_of(jnp.concatenate(partial_rows, axis=1)))
        for e in range(N_EXP):
            send_back[half, e] = ordered[e * per : (e + 1) * per, :]
        for step in range(1, N_EXP):
            back(half, step).start()
        got_back[half, me] = send_back[half, me]
    for half in range(HALVES):
        each_step(lambda step: back(half, step).wait_recv())
        returned = whole_of(reorder(to_work, got_back[half].reshape(lines, width // PIECES)))
        over = (((0,), (0,)), ((), ()))
        sum_ref[:, half * width : (half + 1) * width] = (
            lax.dot_general(combine_hi, returned, over, preferred_element_type=jnp.float32)
            + lax.dot_general(combine_lo, returned, over, preferred_element_type=jnp.float32)
        ).astype(jnp.bfloat16)

    def finish(pair, _):
        for odd in (0, 1):
            chunk = pair * 2 + odd
            for half in range(2):
                copy1(chunk, odd, half).wait_send()
                copy2(chunk, odd, half).wait_send()
            for step in range(1, 4):
                copy3(chunk, odd, step).wait_send()
        each_step(lambda step: there(pair, step).wait_send())
        return 0

    lax.fori_loop(0, CHUNKS // 2, finish, 0)
    each_step(lambda step: norms(step).wait_send())
    for half in range(HALVES):
        each_step(lambda step: back(half, step).wait_send())


def on_device_fused(
    hidden_in,
    queries,
    keys,
    values,
    out_proj,
    norm_gain,
    expert_ids,
    gate_fixed,
    live_counts,
    gate_proj,
    up_proj,
    down_proj,
):
    bf16 = jnp.bfloat16
    dma = pltpu.SemaphoreType.DMA
    vmem = pl.BlockSpec(memory_space=pltpu.VMEM)
    hbm = pl.BlockSpec(memory_space=pl.ANY)
    going = pltpu.VMEM((D // PAIR, N_EXP, CAP * PIECES, PAIR // PIECES), bf16)
    coming = pltpu.VMEM((HALVES, N_EXP, CAP * PIECES, D // HALVES // PIECES), bf16)
    norm_tiles = pltpu.VMEM((1, N_EXP, 8, 128), jnp.float32)
    return pl.pallas_call(
        fused_kernel,
        out_shape=(pltpu.VMEM((ROWS, D), bf16), pltpu.VMEM((ROWS, D), bf16)),
        in_specs=[vmem] * 7 + [pl.BlockSpec(memory_space=pltpu.SMEM)] + [hbm] * 4,
        out_specs=(vmem, vmem),
        scratch_shapes=[
            pltpu.VMEM((HEAD_COLS, D), bf16),
            pltpu.VMEM((D, FF), bf16),
            pltpu.VMEM((D, FF), bf16),
            pltpu.VMEM((FF, D), bf16),
            pltpu.VMEM((SEQ, HEAD_COLS), bf16),
            pltpu.VMEM((CHUNKS, 2, 2, 2, 2, ROWS, WIDE), bf16),
            pltpu.VMEM((CHUNKS, 2, 2, 2, ROWS, WIDE), bf16),
            pltpu.VMEM((CHUNKS, 2, 2, ROWS, WIDE), bf16),
            pltpu.VMEM((CHUNKS, 3, ROWS, WIDE), bf16),
            pltpu.VMEM((SLOTS, FF), jnp.float32),
            pltpu.VMEM((SLOTS, FF), jnp.float32),
            pltpu.VMEM((SLOTS, FF), bf16),
            going,
            going,
            coming,
            coming,
            norm_tiles,
            norm_tiles,
            dma((4,)),
            dma((CHUNKS, 2)),
            dma((CHUNKS, 2)),
            dma((CHUNKS, 2)),
            dma((CHUNKS, 2)),
            dma((CHUNKS, 3)),
            dma((CHUNKS, 3)),
            dma((D // PAIR, N_EXP - 1)),
            dma((D // PAIR, N_EXP - 1)),
            dma((HALVES, N_EXP - 1)),
            dma((HALVES, N_EXP - 1)),
            dma((1, N_EXP - 1)),
            dma((1, N_EXP - 1)),
        ],
        compiler_params=pltpu.CompilerParams(
            collective_id=0, has_side_effects=True, vmem_limit_bytes=56 * 2**20
        ),
        name="decoder_layer",
    )(
        hidden_in,
        queries,
        keys,
        values,
        norm_gain.reshape(1, D),
        expert_ids.T,
        gate_fixed.T,
        live_counts,
        out_proj,
        gate_proj,
        up_proj,
        down_proj,
    )


def on_device_general(
    hidden_in,
    queries,
    keys,
    values,
    out_proj,
    norm_gain,
    expert_ids,
    gate_fixed,
    live_counts,
    gate_proj,
    up_proj,
    down_proj,
):
    n_ctx = lax.axis_size("ctx")
    n_exp = lax.axis_size("exp")
    seq_rows = queries.shape[0]
    local_heads = queries.shape[1] // HEAD_DIM
    group = HEADS // KV_HEADS
    kv_index = lax.axis_index("exp") * local_heads // group
    key_head = lax.dynamic_slice_in_dim(keys, kv_index * HEAD_DIM, HEAD_DIM, 1)
    value_head = lax.dynamic_slice_in_dim(values, kv_index * HEAD_DIM, HEAD_DIM, 1)
    query_heads = queries.reshape(seq_rows, local_heads, HEAD_DIM).transpose(1, 0, 2)
    query_pos = lax.axis_index("ctx") * seq_rows + jnp.arange(seq_rows, dtype=jnp.int32)
    scale = HEAD_DIM ** (-0.5)

    def update(carry, key_block, value_block, first):
        running, total, accum = carry
        scores = (
            jnp.einsum("hqd,kd->hqk", query_heads, key_block, preferred_element_type=jnp.float32)
            * scale
        )
        key_pos = first + jnp.arange(seq_rows, dtype=jnp.int32)
        visible = (key_pos[None, :] <= query_pos[:, None])[None]
        scores = jnp.where(visible, scores, -1e30)
        newest = jnp.maximum(running, jnp.max(scores, axis=2))
        weights = jnp.where(visible, jnp.exp(scores - newest[..., None]), 0.0)
        factor = jnp.exp(running - newest)
        total = total * factor + jnp.sum(weights, axis=2)
        accum = accum * factor[..., None] + jnp.einsum(
            "hqk,kd->hqd",
            weights.astype(jnp.bfloat16),
            value_block,
            preferred_element_type=jnp.float32,
        )
        return (newest, total, accum)

    start_state = (
        jnp.full((local_heads, seq_rows), -1e30, jnp.float32),
        jnp.zeros((local_heads, seq_rows), jnp.float32),
        jnp.zeros((local_heads, seq_rows, HEAD_DIM), jnp.float32),
    )
    carry = start_state
    key_piece = lax.all_gather(key_head, "ctx", axis=0, tiled=True)
    value_piece = lax.all_gather(value_head, "ctx", axis=0, tiled=True)
    blocks = key_piece.shape[0] // seq_rows
    key_blocks = key_piece.reshape(blocks, seq_rows, HEAD_DIM)
    value_blocks = value_piece.reshape(blocks, seq_rows, HEAD_DIM)
    firsts = jnp.arange(blocks, dtype=jnp.int32) * seq_rows

    def step(state, inputs):
        key_block, value_block, first = inputs
        state = update(state, key_block, value_block, first)
        return (state, None)

    carry, _ = lax.scan(step, carry, (key_blocks, value_blocks, firsts))
    running, total, accum = carry
    attended = (
        (accum / total[..., None])
        .astype(jnp.bfloat16)
        .transpose(1, 0, 2)
        .reshape(seq_rows, local_heads * HEAD_DIM)
    )
    token_rows = hidden_in.shape[0]
    attn_out = lax.psum_scatter(
        jnp.dot(attended, out_proj, preferred_element_type=jnp.float32).astype(jnp.bfloat16),
        "exp",
        scatter_dimension=0,
        tiled=True,
    ).astype(jnp.float32)
    residual = hidden_in.astype(jnp.float32) + attn_out
    mixed = residual.astype(jnp.bfloat16)
    norm_scale = lax.rsqrt(jnp.mean(residual * residual, axis=1, keepdims=True) + 1e-06)
    normed = (residual * norm_scale * norm_gain).astype(jnp.bfloat16)
    slot_count = n_exp * CAP
    live = jnp.arange(token_rows, dtype=jnp.int32) < live_counts[0]
    active = (expert_ids < n_exp) & live[:, None]
    onehot = (
        (expert_ids[..., None] == jnp.arange(n_exp, dtype=jnp.int32)) & active[..., None]
    ).astype(jnp.int32)
    onehot = onehot.reshape(token_rows * TOPK, n_exp)
    earlier = jnp.cumsum(onehot, axis=0) - onehot
    rank = jnp.sum(earlier * onehot, axis=1).reshape(token_rows, TOPK)
    slot = jnp.where(active, expert_ids * CAP + rank, -1)
    pair_hit = slot[..., None] == jnp.arange(slot_count, dtype=jnp.int32)
    dispatch = jnp.any(pair_hit, axis=1).astype(jnp.bfloat16)
    send = jnp.einsum("rs,rd->sd", dispatch, normed, preferred_element_type=jnp.float32).astype(
        jnp.bfloat16
    )
    send = send.reshape(n_exp, CAP, D)
    route_weights = gate_fixed.astype(jnp.float32) / 4096.0
    combine = jnp.sum(pair_hit.astype(jnp.float32) * route_weights[..., None], axis=1)
    copies = jnp.broadcast_to(send[None], (n_ctx, n_exp, CAP, D)).reshape(n_ctx * n_exp, CAP, D)
    rows3 = lax.all_to_all(copies, ("ctx", "exp"), split_axis=0, concat_axis=0, tiled=True)
    flat_rows = rows3.reshape(-1, D)
    gate_part = jnp.dot(flat_rows, gate_proj[0], preferred_element_type=jnp.float32)
    up_part = jnp.dot(flat_rows, up_proj[0], preferred_element_type=jnp.float32)
    hidden = (jax.nn.silu(gate_part) * up_part).astype(jnp.bfloat16)
    partial_value = jnp.dot(hidden, down_proj[0], preferred_element_type=jnp.float32)
    partial_value = partial_value.reshape(rows3.shape[0], rows3.shape[1], D).astype(jnp.bfloat16)
    returned = lax.all_to_all(
        partial_value, ("ctx", "exp"), split_axis=0, concat_axis=0, tiled=True
    )
    expert_out = (
        returned.astype(jnp.float32).reshape(n_ctx, slot_count, D).sum(axis=0).astype(jnp.bfloat16)
    )
    expert_sum = jnp.dot(combine, expert_out.astype(jnp.float32), precision=lax.Precision.HIGHEST)
    return (mixed, expert_sum.astype(jnp.bfloat16))


def solution(mesh):
    in_specs = (
        P(("rep", "ctx", "exp"), None),
        P(("rep", "ctx"), "exp"),
        P(("rep", "ctx"), None),
        P(("rep", "ctx"), None),
        P("exp", None),
        P(),
        P(("rep", "ctx", "exp"), None),
        P(("rep", "ctx", "exp"), None),
        P(("rep", "ctx", "exp")),
        P("exp", None, "ctx"),
        P("exp", None, "ctx"),
        P("exp", "ctx", None),
    )
    out_specs = (P(("rep", "ctx", "exp"), None), P(("rep", "ctx", "exp"), None))
    sizes = mesh.shape
    fused = sizes["ctx"] == 1 and sizes["exp"] == N_EXP
    body = on_device_fused if fused else on_device_general
    return jax.shard_map(
        body, mesh=mesh, in_specs=in_specs, out_specs=out_specs, check_vma=False
    )
```

```python
import jax
import jax.numpy as jnp
from jax import lax
from jax.experimental import pallas as pl
from jax.experimental.pallas import tpu as pltpu
from jax.sharding import PartitionSpec as P

D = 4096
HEADS = 64
KV_HEADS = 4
HEAD_DIM = 128
TOPK = 8
CAP = 2


N_EXP = 16
ROWS = 32
SEQ = N_EXP * ROWS
HEAD_COLS = 512
FF = 1536
WIDE = 512
CHUNKS = D // WIDE
SLOTS = N_EXP * CAP
QBLOCK = 256
PIECES = 8
PAIR = 2 * WIDE
HALVES = 2


def fused_kernel(
    hidden_ref,
    q_ref,
    k_ref,
    v_ref,
    gain_ref,
    ids_ref,
    fixed_ref,
    live_ref,
    proj_hbm,
    gate_hbm,
    up_hbm,
    down_hbm,
    mixed_ref,
    sum_ref,
    proj,
    gate,
    up,
    down,
    attended,
    part,
    got1,
    got2,
    got3,
    gate_sum,
    up_sum,
    hid,
    send_rows,
    got_rows,
    send_back,
    got_back,
    send_norm,
    got_norm,
    load_sem,
    send1,
    recv1,
    send2,
    recv2,
    send3,
    recv3,
    send4,
    recv4,
    send5,
    recv5,
    send6,
    recv6,
):
    me = lax.axis_index("exp")
    x, y, z = me % 2, (me // 2) % 2, me // 4
    load_proj = pltpu.make_async_copy(proj_hbm, proj, load_sem.at[0])
    load_gate = pltpu.make_async_copy(gate_hbm.at[0], gate, load_sem.at[1])

    def load_up(piece):
        deep = slice(piece * PAIR, (piece + 1) * PAIR)
        return pltpu.make_async_copy(up_hbm.at[0, deep], up.at[deep], load_sem.at[2 + piece])

    def load_down(piece):
        deep = slice(piece * (FF // 4), (piece + 1) * (FF // 4))
        return pltpu.make_async_copy(down_hbm.at[0, deep], down.at[deep], load_sem.at[6 + piece])

    load_proj.start()
    load_gate.start()

    barrier = pltpu.get_barrier_semaphore()
    for step in range(1, N_EXP):
        pl.semaphore_signal(
            barrier,
            inc=1,
            device_id={"exp": (me + step) % N_EXP},
            device_id_type=pl.DeviceIdType.MESH,
        )

    kv = (me * (HEAD_COLS // HEAD_DIM)) // (HEADS // KV_HEADS)
    kv_cols = pl.ds(pl.multiple_of(kv * HEAD_DIM, HEAD_DIM), HEAD_DIM)
    scale = HEAD_DIM ** (-0.5)
    for block in range(SEQ // QBLOCK):
        first = block * QBLOCK
        keys_seen = first + QBLOCK
        q_pos = first + lax.broadcasted_iota(jnp.int32, (QBLOCK, keys_seen), 0)
        k_pos = lax.broadcasted_iota(jnp.int32, (QBLOCK, keys_seen), 1)
        visible = k_pos <= q_pos
        for head in range(HEAD_COLS // HEAD_DIM):
            cols = slice(head * HEAD_DIM, (head + 1) * HEAD_DIM)
            scores = (
                lax.dot_general(
                    q_ref[first : first + QBLOCK, cols],
                    k_ref[:keys_seen, kv_cols],
                    (((1,), (1,)), ((), ())),
                    preferred_element_type=jnp.float32,
                )
                * scale
            )
            scores = jnp.where(visible, scores, -1e30)
            largest = jnp.max(scores, axis=1, keepdims=True)
            weights = jnp.exp(scores - largest)
            total = jnp.sum(weights, axis=1, keepdims=True)
            summed = jnp.dot(
                weights.astype(jnp.bfloat16),
                v_ref[:keys_seen, kv_cols],
                preferred_element_type=jnp.float32,
            )
            attended[first : first + QBLOCK, cols] = (summed / total).astype(jnp.bfloat16)

    load_proj.wait()
    pl.semaphore_wait(barrier, N_EXP - 1)

    x_peer, y_peer = me + 1 - 2 * x, me + 2 - 4 * y

    def places(odd):
        return (y, x, y_peer, x_peer) if odd else (x, y, x_peer, y_peer)

    def copy1(chunk, odd):
        a, _, peer, _ = places(odd)
        return pltpu.make_async_remote_copy(
            src_ref=part.at[chunk, 1 - a],
            dst_ref=got1.at[chunk],
            send_sem=send1.at[chunk],
            recv_sem=recv1.at[chunk],
            device_id={"exp": peer},
            device_id_type=pl.DeviceIdType.MESH,
        )

    def copy2(chunk, odd):
        a, b, _, peer = places(odd)
        return pltpu.make_async_remote_copy(
            src_ref=part.at[chunk, a, 1 - b],
            dst_ref=got2.at[chunk],
            send_sem=send2.at[chunk],
            recv_sem=recv2.at[chunk],
            device_id={"exp": peer},
            device_id_type=pl.DeviceIdType.MESH,
        )

    def copy3(chunk, odd, step):
        a, b, _, _ = places(odd)
        other = (z + step) % 4
        return pltpu.make_async_remote_copy(
            src_ref=part.at[chunk, a, b, other],
            dst_ref=got3.at[chunk, step - 1],
            send_sem=send3.at[chunk, step - 1],
            recv_sem=recv3.at[chunk, step - 1],
            device_id={"exp": me + (other - z) * 4},
            device_id_type=pl.DeviceIdType.MESH,
        )

    def project(pair):
        for odd in (0, 1):
            chunk = pair * 2 + odd
            cols = slice(chunk * WIDE, (chunk + 1) * WIDE)
            for half in range(2):
                lines = SEQ // 2
                product = jnp.dot(
                    attended[half * lines : (half + 1) * lines, :],
                    proj[:, cols],
                    preferred_element_type=jnp.float32,
                ).astype(jnp.bfloat16)
                for local in range(N_EXP // 2):
                    owner = half * (N_EXP // 2) + local
                    ox, oy, oz = owner % 2, (owner // 2) % 2, owner // 4
                    a, b = (oy, ox) if odd else (ox, oy)
                    part[chunk, a, b, oz] = product[local * ROWS : (local + 1) * ROWS, :]
            copy1(chunk, odd).start()

    def fold1(pair):
        for odd in (0, 1):
            chunk = pair * 2 + odd
            a = places(odd)[0]
            copy1(chunk, odd).wait_recv()
            for b in range(2):
                for c in range(4):
                    part[chunk, a, b, c] = part[chunk, a, b, c] + got1[chunk, b, c]
            copy2(chunk, odd).start()

    def fold2(pair):
        for odd in (0, 1):
            chunk = pair * 2 + odd
            a, b, _, _ = places(odd)
            copy2(chunk, odd).wait_recv()
            for c in range(4):
                part[chunk, a, b, c] = part[chunk, a, b, c] + got2[chunk, c]
            for step in range(1, 4):
                copy3(chunk, odd, step).start()

    project(0)
    project(1)

    slot = lax.broadcasted_iota(jnp.int32, (SLOTS, ROWS), 0)
    row = lax.broadcasted_iota(jnp.int32, (SLOTS, ROWS), 1)
    weight = jnp.zeros((SLOTS, ROWS), jnp.int32)
    named = jnp.zeros((SLOTS, ROWS), jnp.float32)
    for k in range(TOPK):
        same = (ids_ref[k : k + 1, :] == slot // CAP) & (row < live_ref[0])
        weight = weight + jnp.where(same, fixed_ref[k : k + 1, :], 0)
        named = named + jnp.where(same, 1.0, 0.0)
    before = lax.broadcasted_iota(jnp.int32, (ROWS, ROWS), 0) < lax.broadcasted_iota(
        jnp.int32, (ROWS, ROWS), 1
    )
    earlier = jnp.dot(
        named.astype(jnp.bfloat16),
        jnp.where(before, 1.0, 0.0).astype(jnp.bfloat16),
        preferred_element_type=jnp.float32,
    )
    taken = (named > 0.5) & (jnp.abs(earlier - (slot % CAP).astype(jnp.float32)) < 0.5)
    dispatch_exact = jnp.where(taken, 1.0, 0.0)
    dispatch = dispatch_exact.astype(jnp.bfloat16)
    weight = jnp.where(taken, weight, 0)
    coarse = (weight // 64) * 64
    combine_hi = (coarse.astype(jnp.float32) / 4096.0).astype(jnp.bfloat16)
    combine_lo = ((weight - coarse).astype(jnp.float32) / 4096.0).astype(jnp.bfloat16)

    lines = SLOTS * PIECES
    per = CAP * PIECES
    i = lax.broadcasted_iota(jnp.int32, (lines, lines), 0)
    j = lax.broadcasted_iota(jnp.int32, (lines, lines), 1)
    to_work = jnp.where((i % SLOTS) * PIECES + i // SLOTS == j, 1.0, 0.0).astype(jnp.bfloat16)
    to_travel = jnp.where((j % SLOTS) * PIECES + j // SLOTS == i, 1.0, 0.0).astype(jnp.bfloat16)

    def reorder(matrix, value):
        return jnp.dot(matrix, value, preferred_element_type=jnp.float32).astype(jnp.bfloat16)

    def pieces_of(value):
        width = value.shape[1] // PIECES
        return jnp.concatenate(
            [value[:, p * width : (p + 1) * width] for p in range(PIECES)], axis=0
        )

    def whole_of(value):
        return jnp.concatenate(
            [value[p * SLOTS : (p + 1) * SLOTS, :] for p in range(PIECES)], axis=1
        )

    def exchange(source, target, send_sem, recv_sem, part_index, step):
        other = (me + step) % N_EXP
        return pltpu.make_async_remote_copy(
            src_ref=source.at[part_index, other],
            dst_ref=target.at[part_index, me],
            send_sem=send_sem.at[part_index, step - 1],
            recv_sem=recv_sem.at[part_index, step - 1],
            device_id={"exp": other},
            device_id_type=pl.DeviceIdType.MESH,
        )

    def there(pair, step):
        return exchange(send_rows, got_rows, send4, recv4, pair, step)

    def back(half, step):
        return exchange(send_back, got_back, send5, recv5, half, step)

    def norms(step):
        return exchange(send_norm, got_norm, send6, recv6, 0, step)

    def each_step(action):
        def body(step, _):
            action(step)
            return 0

        lax.fori_loop(1, N_EXP, body, 0)

    squares = [jnp.zeros((ROWS, 1), jnp.float32)]

    def final(pair):
        picked = []
        for odd in (0, 1):
            chunk = pair * 2 + odd
            a, b, _, _ = places(odd)
            for step in range(1, 4):
                copy3(chunk, odd, step).wait_recv()
            cols = slice(chunk * WIDE, (chunk + 1) * WIDE)
            total = part[chunk, a, b, z].astype(jnp.float32)
            for step in range(3):
                total = total + got3[chunk, step].astype(jnp.float32)
            total = total + hidden_ref[:, cols].astype(jnp.float32)
            mixed_ref[:, cols] = total.astype(jnp.bfloat16)
            squares[0] = squares[0] + jnp.sum(total * total, axis=1, keepdims=True)
            gained = (total * gain_ref[:, cols]).astype(jnp.bfloat16)
            picked.append(reorder(dispatch, gained))
        ordered = reorder(to_travel, pieces_of(jnp.concatenate(picked, axis=1)))
        for e in range(N_EXP):
            send_rows[pair, e] = ordered[e * per : (e + 1) * per, :]
        each_step(lambda step: there(pair, step).start())
        got_rows[pair, me] = send_rows[pair, me]

    def send_norms():
        norm = lax.rsqrt(squares[0] / D + 1e-06)
        wide = jnp.broadcast_to(norm, (ROWS, 128))
        slot_norm = jnp.dot(
            dispatch_exact, wide, precision=lax.Precision.HIGHEST, preferred_element_type=jnp.float32
        )
        line = lax.broadcasted_iota(jnp.int32, (N_EXP * 8, SLOTS), 0)
        source = lax.broadcasted_iota(jnp.int32, (N_EXP * 8, SLOTS), 1)
        spread = jnp.where((line // 8) * CAP + line % CAP == source, 1.0, 0.0)
        tiles = jnp.dot(
            spread, slot_norm, precision=lax.Precision.HIGHEST, preferred_element_type=jnp.float32
        )
        for e in range(N_EXP):
            send_norm[0, e] = tiles[e * 8 : (e + 1) * 8, :]
        each_step(lambda step: norms(step).start())
        got_norm[0, me] = send_norm[0, me]

    def receive_norms():
        each_step(lambda step: norms(step).wait_recv())
        line = lax.broadcasted_iota(jnp.int32, (SLOTS, N_EXP * 8), 1)
        target = lax.broadcasted_iota(jnp.int32, (SLOTS, N_EXP * 8), 0)
        gather = jnp.where((target // CAP) * 8 + target % CAP == line, 1.0, 0.0)
        return jnp.dot(
            gather,
            got_norm[0].reshape(N_EXP * 8, 128),
            precision=lax.Precision.HIGHEST,
            preferred_element_type=jnp.float32,
        )[:, :1]

    def expert_in(pair):
        if pair == 0:
            load_gate.wait()
        load_up(pair).wait()
        each_step(lambda step: there(pair, step).wait_recv())
        tokens = whole_of(reorder(to_work, got_rows[pair].reshape(lines, PAIR // PIECES)))
        deep = slice(pair * PAIR, (pair + 1) * PAIR)
        for block in range(FF // 512):
            cols = slice(block * 512, (block + 1) * 512)
            for weights_in, sums in ((gate, gate_sum), (up, up_sum)):
                term = jnp.dot(tokens, weights_in[deep, cols], preferred_element_type=jnp.float32)
                sums[:, cols] = term if pair == 0 else sums[:, cols] + term

    load_up(0).start()
    fold1(0)
    project(2)
    load_up(1).start()
    fold1(1)
    fold2(0)
    load_up(2).start()
    project(3)
    load_up(3).start()
    fold1(2)
    fold2(1)
    load_down(0).start()
    final(0)
    load_down(1).start()
    fold1(3)
    fold2(2)
    load_down(2).start()
    final(1)
    load_down(3).start()
    expert_in(0)
    fold2(3)
    final(2)
    expert_in(1)
    final(3)
    send_norms()
    expert_in(2)
    expert_in(3)
    slot_scale = receive_norms()
    for block in range(FF // 512):
        cols = slice(block * 512, (block + 1) * 512)
        gate_part = gate_sum[:, cols] * slot_scale
        up_part = up_sum[:, cols] * slot_scale
        hid[:, cols] = (gate_part / (1.0 + jnp.exp(-gate_part)) * up_part).astype(jnp.bfloat16)

    for piece in range(4):
        load_down(piece).wait()
    width = D // HALVES
    for half in range(HALVES):
        partial_rows = []
        for block in range(width // WIDE):
            first = half * width + block * WIDE
            partial_rows.append(
                jnp.dot(
                    hid[...], down[:, first : first + WIDE], preferred_element_type=jnp.float32
                ).astype(jnp.bfloat16)
            )
        ordered = reorder(to_travel, pieces_of(jnp.concatenate(partial_rows, axis=1)))
        for e in range(N_EXP):
            send_back[half, e] = ordered[e * per : (e + 1) * per, :]
        for step in range(1, N_EXP):
            back(half, step).start()
        got_back[half, me] = send_back[half, me]
    for half in range(HALVES):
        each_step(lambda step: back(half, step).wait_recv())
        returned = whole_of(reorder(to_work, got_back[half].reshape(lines, width // PIECES)))
        over = (((0,), (0,)), ((), ()))
        sum_ref[:, half * width : (half + 1) * width] = (
            lax.dot_general(combine_hi, returned, over, preferred_element_type=jnp.float32)
            + lax.dot_general(combine_lo, returned, over, preferred_element_type=jnp.float32)
        ).astype(jnp.bfloat16)

    def finish(pair, _):
        for odd in (0, 1):
            chunk = pair * 2 + odd
            copy1(chunk, odd).wait_send()
            copy2(chunk, odd).wait_send()
            for step in range(1, 4):
                copy3(chunk, odd, step).wait_send()
        each_step(lambda step: there(pair, step).wait_send())
        return 0

    lax.fori_loop(0, CHUNKS // 2, finish, 0)
    each_step(lambda step: norms(step).wait_send())
    for half in range(HALVES):
        each_step(lambda step: back(half, step).wait_send())


def on_device_fused(
    hidden_in,
    queries,
    keys,
    values,
    out_proj,
    norm_gain,
    expert_ids,
    gate_fixed,
    live_counts,
    gate_proj,
    up_proj,
    down_proj,
):
    bf16 = jnp.bfloat16
    dma = pltpu.SemaphoreType.DMA
    vmem = pl.BlockSpec(memory_space=pltpu.VMEM)
    hbm = pl.BlockSpec(memory_space=pl.ANY)
    going = pltpu.VMEM((D // PAIR, N_EXP, CAP * PIECES, PAIR // PIECES), bf16)
    coming = pltpu.VMEM((HALVES, N_EXP, CAP * PIECES, D // HALVES // PIECES), bf16)
    norm_tiles = pltpu.VMEM((1, N_EXP, 8, 128), jnp.float32)
    return pl.pallas_call(
        fused_kernel,
        out_shape=(pltpu.VMEM((ROWS, D), bf16), pltpu.VMEM((ROWS, D), bf16)),
        in_specs=[vmem] * 7 + [pl.BlockSpec(memory_space=pltpu.SMEM)] + [hbm] * 4,
        out_specs=(vmem, vmem),
        scratch_shapes=[
            pltpu.VMEM((HEAD_COLS, D), bf16),
            pltpu.VMEM((D, FF), bf16),
            pltpu.VMEM((D, FF), bf16),
            pltpu.VMEM((FF, D), bf16),
            pltpu.VMEM((SEQ, HEAD_COLS), bf16),
            pltpu.VMEM((CHUNKS, 2, 2, 4, ROWS, WIDE), bf16),
            pltpu.VMEM((CHUNKS, 2, 4, ROWS, WIDE), bf16),
            pltpu.VMEM((CHUNKS, 4, ROWS, WIDE), bf16),
            pltpu.VMEM((CHUNKS, 3, ROWS, WIDE), bf16),
            pltpu.VMEM((SLOTS, FF), jnp.float32),
            pltpu.VMEM((SLOTS, FF), jnp.float32),
            pltpu.VMEM((SLOTS, FF), bf16),
            going,
            going,
            coming,
            coming,
            norm_tiles,
            norm_tiles,
            dma((10,)),
            dma((CHUNKS,)),
            dma((CHUNKS,)),
            dma((CHUNKS,)),
            dma((CHUNKS,)),
            dma((CHUNKS, 3)),
            dma((CHUNKS, 3)),
            dma((D // PAIR, N_EXP - 1)),
            dma((D // PAIR, N_EXP - 1)),
            dma((HALVES, N_EXP - 1)),
            dma((HALVES, N_EXP - 1)),
            dma((1, N_EXP - 1)),
            dma((1, N_EXP - 1)),
        ],
        compiler_params=pltpu.CompilerParams(
            collective_id=0, has_side_effects=True, vmem_limit_bytes=56 * 2**20
        ),
        name="decoder_layer",
    )(
        hidden_in,
        queries,
        keys,
        values,
        norm_gain.reshape(1, D),
        expert_ids.T,
        gate_fixed.T,
        live_counts,
        out_proj,
        gate_proj,
        up_proj,
        down_proj,
    )


def on_device_general(
    hidden_in,
    queries,
    keys,
    values,
    out_proj,
    norm_gain,
    expert_ids,
    gate_fixed,
    live_counts,
    gate_proj,
    up_proj,
    down_proj,
):
    n_ctx = lax.axis_size("ctx")
    n_exp = lax.axis_size("exp")
    seq_rows = queries.shape[0]
    local_heads = queries.shape[1] // HEAD_DIM
    group = HEADS // KV_HEADS
    kv_index = lax.axis_index("exp") * local_heads // group
    key_head = lax.dynamic_slice_in_dim(keys, kv_index * HEAD_DIM, HEAD_DIM, 1)
    value_head = lax.dynamic_slice_in_dim(values, kv_index * HEAD_DIM, HEAD_DIM, 1)
    query_heads = queries.reshape(seq_rows, local_heads, HEAD_DIM).transpose(1, 0, 2)
    query_pos = lax.axis_index("ctx") * seq_rows + jnp.arange(seq_rows, dtype=jnp.int32)
    scale = HEAD_DIM ** (-0.5)

    def update(carry, key_block, value_block, first):
        running, total, accum = carry
        scores = (
            jnp.einsum("hqd,kd->hqk", query_heads, key_block, preferred_element_type=jnp.float32)
            * scale
        )
        key_pos = first + jnp.arange(seq_rows, dtype=jnp.int32)
        visible = (key_pos[None, :] <= query_pos[:, None])[None]
        scores = jnp.where(visible, scores, -1e30)
        newest = jnp.maximum(running, jnp.max(scores, axis=2))
        weights = jnp.where(visible, jnp.exp(scores - newest[..., None]), 0.0)
        factor = jnp.exp(running - newest)
        total = total * factor + jnp.sum(weights, axis=2)
        accum = accum * factor[..., None] + jnp.einsum(
            "hqk,kd->hqd",
            weights.astype(jnp.bfloat16),
            value_block,
            preferred_element_type=jnp.float32,
        )
        return (newest, total, accum)

    start_state = (
        jnp.full((local_heads, seq_rows), -1e30, jnp.float32),
        jnp.zeros((local_heads, seq_rows), jnp.float32),
        jnp.zeros((local_heads, seq_rows, HEAD_DIM), jnp.float32),
    )
    carry = start_state
    key_piece = lax.all_gather(key_head, "ctx", axis=0, tiled=True)
    value_piece = lax.all_gather(value_head, "ctx", axis=0, tiled=True)
    blocks = key_piece.shape[0] // seq_rows
    key_blocks = key_piece.reshape(blocks, seq_rows, HEAD_DIM)
    value_blocks = value_piece.reshape(blocks, seq_rows, HEAD_DIM)
    firsts = jnp.arange(blocks, dtype=jnp.int32) * seq_rows

    def step(state, inputs):
        key_block, value_block, first = inputs
        state = update(state, key_block, value_block, first)
        return (state, None)

    carry, _ = lax.scan(step, carry, (key_blocks, value_blocks, firsts))
    running, total, accum = carry
    attended = (
        (accum / total[..., None])
        .astype(jnp.bfloat16)
        .transpose(1, 0, 2)
        .reshape(seq_rows, local_heads * HEAD_DIM)
    )
    token_rows = hidden_in.shape[0]
    attn_out = lax.psum_scatter(
        jnp.dot(attended, out_proj, preferred_element_type=jnp.float32).astype(jnp.bfloat16),
        "exp",
        scatter_dimension=0,
        tiled=True,
    ).astype(jnp.float32)
    residual = hidden_in.astype(jnp.float32) + attn_out
    mixed = residual.astype(jnp.bfloat16)
    norm_scale = lax.rsqrt(jnp.mean(residual * residual, axis=1, keepdims=True) + 1e-06)
    normed = (residual * norm_scale * norm_gain).astype(jnp.bfloat16)
    slot_count = n_exp * CAP
    live = jnp.arange(token_rows, dtype=jnp.int32) < live_counts[0]
    active = (expert_ids < n_exp) & live[:, None]
    onehot = (
        (expert_ids[..., None] == jnp.arange(n_exp, dtype=jnp.int32)) & active[..., None]
    ).astype(jnp.int32)
    onehot = onehot.reshape(token_rows * TOPK, n_exp)
    earlier = jnp.cumsum(onehot, axis=0) - onehot
    rank = jnp.sum(earlier * onehot, axis=1).reshape(token_rows, TOPK)
    slot = jnp.where(active, expert_ids * CAP + rank, -1)
    pair_hit = slot[..., None] == jnp.arange(slot_count, dtype=jnp.int32)
    dispatch = jnp.any(pair_hit, axis=1).astype(jnp.bfloat16)
    send = jnp.einsum("rs,rd->sd", dispatch, normed, preferred_element_type=jnp.float32).astype(
        jnp.bfloat16
    )
    send = send.reshape(n_exp, CAP, D)
    route_weights = gate_fixed.astype(jnp.float32) / 4096.0
    combine = jnp.sum(pair_hit.astype(jnp.float32) * route_weights[..., None], axis=1)
    copies = jnp.broadcast_to(send[None], (n_ctx, n_exp, CAP, D)).reshape(n_ctx * n_exp, CAP, D)
    rows3 = lax.all_to_all(copies, ("ctx", "exp"), split_axis=0, concat_axis=0, tiled=True)
    flat_rows = rows3.reshape(-1, D)
    gate_part = jnp.dot(flat_rows, gate_proj[0], preferred_element_type=jnp.float32)
    up_part = jnp.dot(flat_rows, up_proj[0], preferred_element_type=jnp.float32)
    hidden = (jax.nn.silu(gate_part) * up_part).astype(jnp.bfloat16)
    partial_value = jnp.dot(hidden, down_proj[0], preferred_element_type=jnp.float32)
    partial_value = partial_value.reshape(rows3.shape[0], rows3.shape[1], D).astype(jnp.bfloat16)
    returned = lax.all_to_all(
        partial_value, ("ctx", "exp"), split_axis=0, concat_axis=0, tiled=True
    )
    expert_out = (
        returned.astype(jnp.float32).reshape(n_ctx, slot_count, D).sum(axis=0).astype(jnp.bfloat16)
    )
    expert_sum = jnp.dot(combine, expert_out.astype(jnp.float32), precision=lax.Precision.HIGHEST)
    return (mixed, expert_sum.astype(jnp.bfloat16))


def solution(mesh):
    in_specs = (
        P(("rep", "ctx", "exp"), None),
        P(("rep", "ctx"), "exp"),
        P(("rep", "ctx"), None),
        P(("rep", "ctx"), None),
        P("exp", None),
        P(),
        P(("rep", "ctx", "exp"), None),
        P(("rep", "ctx", "exp"), None),
        P(("rep", "ctx", "exp")),
        P("exp", None, "ctx"),
        P("exp", None, "ctx"),
        P("exp", "ctx", None),
    )
    out_specs = (P(("rep", "ctx", "exp"), None), P(("rep", "ctx", "exp"), None))
    sizes = mesh.shape
    fused = sizes["ctx"] == 1 and sizes["exp"] == N_EXP
    body = on_device_fused if fused else on_device_general
    return jax.shard_map(
        body, mesh=mesh, in_specs=in_specs, out_specs=out_specs, check_vma=False
    )
```

```python
import jax
import jax.numpy as jnp
from jax import lax
from jax.experimental import pallas as pl
from jax.experimental.pallas import tpu as pltpu
from jax.sharding import PartitionSpec as P

D = 4096
HEADS = 64
KV_HEADS = 4
HEAD_DIM = 128
TOPK = 8
CAP = 2


N_EXP = 16
ROWS = 32
SEQ = N_EXP * ROWS
HEAD_COLS = 512
FF = 1536
WIDE = 512
CHUNKS = D // WIDE
SLOTS = N_EXP * CAP
QBLOCK = 256
EARLY = 2
PIECES = 8
PAIR = 2 * WIDE
HALVES = 2


def fused_kernel(
    hidden_ref,
    q_ref,
    k_ref,
    v_ref,
    gain_ref,
    ids_ref,
    fixed_ref,
    live_ref,
    proj_hbm,
    gate_hbm,
    up_hbm,
    down_hbm,
    mixed_ref,
    sum_ref,
    proj,
    gate,
    up,
    down,
    attended,
    part,
    got1,
    got2,
    got3,
    gate_sum,
    up_sum,
    hid,
    send_rows,
    got_rows,
    send_back,
    got_back,
    send_norm,
    got_norm,
    load_sem,
    send1,
    recv1,
    send2,
    recv2,
    send3,
    recv3,
    send4,
    recv4,
    send5,
    recv5,
    send6,
    recv6,
):
    me = lax.axis_index("exp")
    x, y, z = me % 2, (me // 2) % 2, me // 4
    load_proj = pltpu.make_async_copy(proj_hbm, proj, load_sem.at[0])
    load_gate = pltpu.make_async_copy(gate_hbm.at[0], gate, load_sem.at[1])

    def load_up(piece):
        deep = slice(piece * PAIR, (piece + 1) * PAIR)
        return pltpu.make_async_copy(up_hbm.at[0, deep], up.at[deep], load_sem.at[2 + piece])

    def load_down(piece):
        deep = slice(piece * (FF // 4), (piece + 1) * (FF // 4))
        return pltpu.make_async_copy(down_hbm.at[0, deep], down.at[deep], load_sem.at[6 + piece])

    load_proj.start()
    load_gate.start()

    barrier = pltpu.get_barrier_semaphore()
    for step in range(1, N_EXP):
        pl.semaphore_signal(
            barrier,
            inc=1,
            device_id={"exp": (me + step) % N_EXP},
            device_id_type=pl.DeviceIdType.MESH,
        )

    kv = (me * (HEAD_COLS // HEAD_DIM)) // (HEADS // KV_HEADS)
    kv_cols = pl.ds(pl.multiple_of(kv * HEAD_DIM, HEAD_DIM), HEAD_DIM)
    scale = HEAD_DIM ** (-0.5)

    def attend(block):
        first = block * QBLOCK
        keys_seen = first + QBLOCK
        q_pos = first + lax.broadcasted_iota(jnp.int32, (QBLOCK, keys_seen), 0)
        k_pos = lax.broadcasted_iota(jnp.int32, (QBLOCK, keys_seen), 1)
        visible = k_pos <= q_pos
        for head in range(HEAD_COLS // HEAD_DIM):
            cols = slice(head * HEAD_DIM, (head + 1) * HEAD_DIM)
            scores = (
                lax.dot_general(
                    q_ref[first : first + QBLOCK, cols],
                    k_ref[:keys_seen, kv_cols],
                    (((1,), (1,)), ((), ())),
                    preferred_element_type=jnp.float32,
                )
                * scale
            )
            scores = jnp.where(visible, scores, -1e30)
            largest = jnp.max(scores, axis=1, keepdims=True)
            weights = jnp.exp(scores - largest)
            total = jnp.sum(weights, axis=1, keepdims=True)
            summed = jnp.dot(
                weights.astype(jnp.bfloat16),
                v_ref[:keys_seen, kv_cols],
                preferred_element_type=jnp.float32,
            )
            attended[first : first + QBLOCK, cols] = (summed / total).astype(jnp.bfloat16)

    x_peer, y_peer = me + 1 - 2 * x, me + 2 - 4 * y

    def places(odd):
        return (y, x, y_peer, x_peer) if odd else (x, y, x_peer, y_peer)

    def copy1(chunk, odd, half=None):
        a, _, peer, _ = places(odd)
        index = 0 if half is None else half
        planes = pl.ds(0, 4) if half is None else pl.ds(half * 2, 2)
        return pltpu.make_async_remote_copy(
            src_ref=part.at[chunk, 1 - a, :, planes],
            dst_ref=got1.at[chunk, :, planes],
            send_sem=send1.at[chunk, index],
            recv_sem=recv1.at[chunk, index],
            device_id={"exp": peer},
            device_id_type=pl.DeviceIdType.MESH,
        )

    def halves_of(pair):
        return (0, 1) if pair < EARLY else (None,)

    def copy2(chunk, odd):
        a, b, _, peer = places(odd)
        return pltpu.make_async_remote_copy(
            src_ref=part.at[chunk, a, 1 - b],
            dst_ref=got2.at[chunk],
            send_sem=send2.at[chunk],
            recv_sem=recv2.at[chunk],
            device_id={"exp": peer},
            device_id_type=pl.DeviceIdType.MESH,
        )

    def copy3(chunk, odd, step):
        a, b, _, _ = places(odd)
        other = (z + step) % 4
        return pltpu.make_async_remote_copy(
            src_ref=part.at[chunk, a, b, other],
            dst_ref=got3.at[chunk, step - 1],
            send_sem=send3.at[chunk, step - 1],
            recv_sem=recv3.at[chunk, step - 1],
            device_id={"exp": me + (other - z) * 4},
            device_id_type=pl.DeviceIdType.MESH,
        )

    def project(pair, half):
        lines = SEQ // 2
        for odd in (0, 1):
            chunk = pair * 2 + odd
            cols = slice(chunk * WIDE, (chunk + 1) * WIDE)
            for block in (0, 1) if half is None else (half,):
                product = jnp.dot(
                    attended[block * lines : (block + 1) * lines, :],
                    proj[:, cols],
                    preferred_element_type=jnp.float32,
                ).astype(jnp.bfloat16)
                for local in range(N_EXP // 2):
                    owner = block * (N_EXP // 2) + local
                    ox, oy, oz = owner % 2, (owner // 2) % 2, owner // 4
                    a, b = (oy, ox) if odd else (ox, oy)
                    part[chunk, a, b, oz] = product[local * ROWS : (local + 1) * ROWS, :]
            copy1(chunk, odd, half).start()

    def fold1(pair):
        for odd in (0, 1):
            chunk = pair * 2 + odd
            a = places(odd)[0]
            for half in halves_of(pair):
                copy1(chunk, odd, half).wait_recv()
            b = places(odd)[1]
            for c in range(4):
                part[chunk, a, 1 - b, c] = part[chunk, a, 1 - b, c] + got1[chunk, 1 - b, c]
            copy2(chunk, odd).start()
            for c in range(4):
                part[chunk, a, b, c] = part[chunk, a, b, c] + got1[chunk, b, c]

    def fold2(pair):
        for odd in (0, 1):
            chunk = pair * 2 + odd
            a, b, _, _ = places(odd)
            copy2(chunk, odd).wait_recv()
            for c in range(4):
                part[chunk, a, b, c] = part[chunk, a, b, c] + got2[chunk, c]
            for step in range(1, 4):
                copy3(chunk, odd, step).start()

    attend(0)
    load_proj.wait()
    pl.semaphore_wait(barrier, N_EXP - 1)
    for pair in range(EARLY):
        project(pair, 0)
    attend(1)
    for pair in range(EARLY):
        project(pair, 1)

    slot = lax.broadcasted_iota(jnp.int32, (SLOTS, ROWS), 0)
    row = lax.broadcasted_iota(jnp.int32, (SLOTS, ROWS), 1)
    weight = jnp.zeros((SLOTS, ROWS), jnp.int32)
    named = jnp.zeros((SLOTS, ROWS), jnp.float32)
    for k in range(TOPK):
        same = (ids_ref[k : k + 1, :] == slot // CAP) & (row < live_ref[0])
        weight = weight + jnp.where(same, fixed_ref[k : k + 1, :], 0)
        named = named + jnp.where(same, 1.0, 0.0)
    before = lax.broadcasted_iota(jnp.int32, (ROWS, ROWS), 0) < lax.broadcasted_iota(
        jnp.int32, (ROWS, ROWS), 1
    )
    earlier = jnp.dot(
        named.astype(jnp.bfloat16),
        jnp.where(before, 1.0, 0.0).astype(jnp.bfloat16),
        preferred_element_type=jnp.float32,
    )
    taken = (named > 0.5) & (jnp.abs(earlier - (slot % CAP).astype(jnp.float32)) < 0.5)
    dispatch_exact = jnp.where(taken, 1.0, 0.0)
    dispatch = dispatch_exact.astype(jnp.bfloat16)
    weight = jnp.where(taken, weight, 0)
    coarse = (weight // 64) * 64
    combine_hi = (coarse.astype(jnp.float32) / 4096.0).astype(jnp.bfloat16)
    combine_lo = ((weight - coarse).astype(jnp.float32) / 4096.0).astype(jnp.bfloat16)

    lines = SLOTS * PIECES
    per = CAP * PIECES
    i = lax.broadcasted_iota(jnp.int32, (lines, lines), 0)
    j = lax.broadcasted_iota(jnp.int32, (lines, lines), 1)
    to_work = jnp.where((i % SLOTS) * PIECES + i // SLOTS == j, 1.0, 0.0).astype(jnp.bfloat16)
    to_travel = jnp.where((j % SLOTS) * PIECES + j // SLOTS == i, 1.0, 0.0).astype(jnp.bfloat16)

    def reorder(matrix, value):
        return jnp.dot(matrix, value, preferred_element_type=jnp.float32).astype(jnp.bfloat16)

    def pieces_of(value):
        width = value.shape[1] // PIECES
        return jnp.concatenate(
            [value[:, p * width : (p + 1) * width] for p in range(PIECES)], axis=0
        )

    def whole_of(value):
        return jnp.concatenate(
            [value[p * SLOTS : (p + 1) * SLOTS, :] for p in range(PIECES)], axis=1
        )

    def exchange(source, target, send_sem, recv_sem, part_index, step):
        other = (me + step) % N_EXP
        return pltpu.make_async_remote_copy(
            src_ref=source.at[part_index, other],
            dst_ref=target.at[part_index, me],
            send_sem=send_sem.at[part_index, step - 1],
            recv_sem=recv_sem.at[part_index, step - 1],
            device_id={"exp": other},
            device_id_type=pl.DeviceIdType.MESH,
        )

    def there(pair, step):
        return exchange(send_rows, got_rows, send4, recv4, pair, step)

    def back(half, step):
        return exchange(send_back, got_back, send5, recv5, half, step)

    def norms(step):
        return exchange(send_norm, got_norm, send6, recv6, 0, step)

    def each_step(action):
        def body(step, _):
            action(step)
            return 0

        lax.fori_loop(1, N_EXP, body, 0)

    squares = [jnp.zeros((ROWS, 1), jnp.float32)]

    def final(pair):
        picked = []
        for odd in (0, 1):
            chunk = pair * 2 + odd
            a, b, _, _ = places(odd)
            for step in range(1, 4):
                copy3(chunk, odd, step).wait_recv()
            cols = slice(chunk * WIDE, (chunk + 1) * WIDE)
            total = part[chunk, a, b, z].astype(jnp.float32)
            for step in range(3):
                total = total + got3[chunk, step].astype(jnp.float32)
            total = total + hidden_ref[:, cols].astype(jnp.float32)
            mixed_ref[:, cols] = total.astype(jnp.bfloat16)
            squares[0] = squares[0] + jnp.sum(total * total, axis=1, keepdims=True)
            gained = (total * gain_ref[:, cols]).astype(jnp.bfloat16)
            picked.append(reorder(dispatch, gained))
        ordered = reorder(to_travel, pieces_of(jnp.concatenate(picked, axis=1)))
        for e in range(N_EXP):
            send_rows[pair, e] = ordered[e * per : (e + 1) * per, :]
        each_step(lambda step: there(pair, step).start())
        got_rows[pair, me] = send_rows[pair, me]

    def send_norms():
        norm = lax.rsqrt(squares[0] / D + 1e-06)
        wide = jnp.broadcast_to(norm, (ROWS, 128))
        slot_norm = jnp.dot(
            dispatch_exact, wide, precision=lax.Precision.HIGHEST, preferred_element_type=jnp.float32
        )
        line = lax.broadcasted_iota(jnp.int32, (N_EXP * 8, SLOTS), 0)
        source = lax.broadcasted_iota(jnp.int32, (N_EXP * 8, SLOTS), 1)
        spread = jnp.where((line // 8) * CAP + line % CAP == source, 1.0, 0.0)
        tiles = jnp.dot(
            spread, slot_norm, precision=lax.Precision.HIGHEST, preferred_element_type=jnp.float32
        )
        for e in range(N_EXP):
            send_norm[0, e] = tiles[e * 8 : (e + 1) * 8, :]
        each_step(lambda step: norms(step).start())
        got_norm[0, me] = send_norm[0, me]

    def receive_norms():
        each_step(lambda step: norms(step).wait_recv())
        line = lax.broadcasted_iota(jnp.int32, (SLOTS, N_EXP * 8), 1)
        target = lax.broadcasted_iota(jnp.int32, (SLOTS, N_EXP * 8), 0)
        gather = jnp.where((target // CAP) * 8 + target % CAP == line, 1.0, 0.0)
        return jnp.dot(
            gather,
            got_norm[0].reshape(N_EXP * 8, 128),
            precision=lax.Precision.HIGHEST,
            preferred_element_type=jnp.float32,
        )[:, :1]

    def expert_in(pair):
        if pair == 0:
            load_gate.wait()
        load_up(pair).wait()
        each_step(lambda step: there(pair, step).wait_recv())
        tokens = whole_of(reorder(to_work, got_rows[pair].reshape(lines, PAIR // PIECES)))
        deep = slice(pair * PAIR, (pair + 1) * PAIR)
        for block in range(FF // 512):
            cols = slice(block * 512, (block + 1) * 512)
            for weights_in, sums in ((gate, gate_sum), (up, up_sum)):
                term = jnp.dot(tokens, weights_in[deep, cols], preferred_element_type=jnp.float32)
                sums[:, cols] = term if pair == 0 else sums[:, cols] + term

    load_up(0).start()
    fold1(0)
    project(2, None)
    load_up(1).start()
    fold1(1)
    fold2(0)
    load_up(2).start()
    project(3, None)
    load_up(3).start()
    fold1(2)
    fold2(1)
    load_down(0).start()
    final(0)
    load_down(1).start()
    fold1(3)
    fold2(2)
    load_down(2).start()
    final(1)
    load_down(3).start()
    expert_in(0)
    fold2(3)
    final(2)
    expert_in(1)
    final(3)
    send_norms()
    expert_in(2)
    expert_in(3)
    slot_scale = receive_norms()
    for block in range(FF // 512):
        cols = slice(block * 512, (block + 1) * 512)
        gate_part = gate_sum[:, cols] * slot_scale
        up_part = up_sum[:, cols] * slot_scale
        hid[:, cols] = (gate_part / (1.0 + jnp.exp(-gate_part)) * up_part).astype(jnp.bfloat16)

    for piece in range(4):
        load_down(piece).wait()
    width = D // HALVES
    for half in range(HALVES):
        partial_rows = []
        for block in range(width // WIDE):
            first = half * width + block * WIDE
            partial_rows.append(
                jnp.dot(
                    hid[...], down[:, first : first + WIDE], preferred_element_type=jnp.float32
                ).astype(jnp.bfloat16)
            )
        ordered = reorder(to_travel, pieces_of(jnp.concatenate(partial_rows, axis=1)))
        for e in range(N_EXP):
            send_back[half, e] = ordered[e * per : (e + 1) * per, :]
        for step in range(1, N_EXP):
            back(half, step).start()
        got_back[half, me] = send_back[half, me]
    for half in range(HALVES):
        each_step(lambda step: back(half, step).wait_recv())
        returned = whole_of(reorder(to_work, got_back[half].reshape(lines, width // PIECES)))
        over = (((0,), (0,)), ((), ()))
        sum_ref[:, half * width : (half + 1) * width] = (
            lax.dot_general(combine_hi, returned, over, preferred_element_type=jnp.float32)
            + lax.dot_general(combine_lo, returned, over, preferred_element_type=jnp.float32)
        ).astype(jnp.bfloat16)

    for pair in range(CHUNKS // 2):
        for odd in (0, 1):
            chunk = pair * 2 + odd
            for half in halves_of(pair):
                copy1(chunk, odd, half).wait_send()
            copy2(chunk, odd).wait_send()
            for step in range(1, 4):
                copy3(chunk, odd, step).wait_send()
        each_step(lambda step: there(pair, step).wait_send())
    each_step(lambda step: norms(step).wait_send())
    for half in range(HALVES):
        each_step(lambda step: back(half, step).wait_send())


def on_device_fused(
    hidden_in,
    queries,
    keys,
    values,
    out_proj,
    norm_gain,
    expert_ids,
    gate_fixed,
    live_counts,
    gate_proj,
    up_proj,
    down_proj,
):
    bf16 = jnp.bfloat16
    dma = pltpu.SemaphoreType.DMA
    vmem = pl.BlockSpec(memory_space=pltpu.VMEM)
    hbm = pl.BlockSpec(memory_space=pl.ANY)
    going = pltpu.VMEM((D // PAIR, N_EXP, CAP * PIECES, PAIR // PIECES), bf16)
    coming = pltpu.VMEM((HALVES, N_EXP, CAP * PIECES, D // HALVES // PIECES), bf16)
    norm_tiles = pltpu.VMEM((1, N_EXP, 8, 128), jnp.float32)
    return pl.pallas_call(
        fused_kernel,
        out_shape=(pltpu.VMEM((ROWS, D), bf16), pltpu.VMEM((ROWS, D), bf16)),
        in_specs=[vmem] * 7 + [pl.BlockSpec(memory_space=pltpu.SMEM)] + [hbm] * 4,
        out_specs=(vmem, vmem),
        scratch_shapes=[
            pltpu.VMEM((HEAD_COLS, D), bf16),
            pltpu.VMEM((D, FF), bf16),
            pltpu.VMEM((D, FF), bf16),
            pltpu.VMEM((FF, D), bf16),
            pltpu.VMEM((SEQ, HEAD_COLS), bf16),
            pltpu.VMEM((CHUNKS, 2, 2, 4, ROWS, WIDE), bf16),
            pltpu.VMEM((CHUNKS, 2, 4, ROWS, WIDE), bf16),
            pltpu.VMEM((CHUNKS, 4, ROWS, WIDE), bf16),
            pltpu.VMEM((CHUNKS, 3, ROWS, WIDE), bf16),
            pltpu.VMEM((SLOTS, FF), jnp.float32),
            pltpu.VMEM((SLOTS, FF), jnp.float32),
            pltpu.VMEM((SLOTS, FF), bf16),
            going,
            going,
            coming,
            coming,
            norm_tiles,
            norm_tiles,
            dma((10,)),
            dma((CHUNKS, 2)),
            dma((CHUNKS, 2)),
            dma((CHUNKS,)),
            dma((CHUNKS,)),
            dma((CHUNKS, 3)),
            dma((CHUNKS, 3)),
            dma((D // PAIR, N_EXP - 1)),
            dma((D // PAIR, N_EXP - 1)),
            dma((HALVES, N_EXP - 1)),
            dma((HALVES, N_EXP - 1)),
            dma((1, N_EXP - 1)),
            dma((1, N_EXP - 1)),
        ],
        compiler_params=pltpu.CompilerParams(
            collective_id=0, has_side_effects=True, vmem_limit_bytes=56 * 2**20
        ),
        name="decoder_layer",
    )(
        hidden_in,
        queries,
        keys,
        values,
        norm_gain.reshape(1, D),
        expert_ids.T,
        gate_fixed.T,
        live_counts,
        out_proj,
        gate_proj,
        up_proj,
        down_proj,
    )


def on_device_general(
    hidden_in,
    queries,
    keys,
    values,
    out_proj,
    norm_gain,
    expert_ids,
    gate_fixed,
    live_counts,
    gate_proj,
    up_proj,
    down_proj,
):
    n_ctx = lax.axis_size("ctx")
    n_exp = lax.axis_size("exp")
    seq_rows = queries.shape[0]
    local_heads = queries.shape[1] // HEAD_DIM
    group = HEADS // KV_HEADS
    kv_index = lax.axis_index("exp") * local_heads // group
    key_head = lax.dynamic_slice_in_dim(keys, kv_index * HEAD_DIM, HEAD_DIM, 1)
    value_head = lax.dynamic_slice_in_dim(values, kv_index * HEAD_DIM, HEAD_DIM, 1)
    query_heads = queries.reshape(seq_rows, local_heads, HEAD_DIM).transpose(1, 0, 2)
    query_pos = lax.axis_index("ctx") * seq_rows + jnp.arange(seq_rows, dtype=jnp.int32)
    scale = HEAD_DIM ** (-0.5)

    def update(carry, key_block, value_block, first):
        running, total, accum = carry
        scores = (
            jnp.einsum("hqd,kd->hqk", query_heads, key_block, preferred_element_type=jnp.float32)
            * scale
        )
        key_pos = first + jnp.arange(seq_rows, dtype=jnp.int32)
        visible = (key_pos[None, :] <= query_pos[:, None])[None]
        scores = jnp.where(visible, scores, -1e30)
        newest = jnp.maximum(running, jnp.max(scores, axis=2))
        weights = jnp.where(visible, jnp.exp(scores - newest[..., None]), 0.0)
        factor = jnp.exp(running - newest)
        total = total * factor + jnp.sum(weights, axis=2)
        accum = accum * factor[..., None] + jnp.einsum(
            "hqk,kd->hqd",
            weights.astype(jnp.bfloat16),
            value_block,
            preferred_element_type=jnp.float32,
        )
        return (newest, total, accum)

    start_state = (
        jnp.full((local_heads, seq_rows), -1e30, jnp.float32),
        jnp.zeros((local_heads, seq_rows), jnp.float32),
        jnp.zeros((local_heads, seq_rows, HEAD_DIM), jnp.float32),
    )
    carry = start_state
    key_piece = lax.all_gather(key_head, "ctx", axis=0, tiled=True)
    value_piece = lax.all_gather(value_head, "ctx", axis=0, tiled=True)
    blocks = key_piece.shape[0] // seq_rows
    key_blocks = key_piece.reshape(blocks, seq_rows, HEAD_DIM)
    value_blocks = value_piece.reshape(blocks, seq_rows, HEAD_DIM)
    firsts = jnp.arange(blocks, dtype=jnp.int32) * seq_rows

    def step(state, inputs):
        key_block, value_block, first = inputs
        state = update(state, key_block, value_block, first)
        return (state, None)

    carry, _ = lax.scan(step, carry, (key_blocks, value_blocks, firsts))
    running, total, accum = carry
    attended = (
        (accum / total[..., None])
        .astype(jnp.bfloat16)
        .transpose(1, 0, 2)
        .reshape(seq_rows, local_heads * HEAD_DIM)
    )
    token_rows = hidden_in.shape[0]
    attn_out = lax.psum_scatter(
        jnp.dot(attended, out_proj, preferred_element_type=jnp.float32).astype(jnp.bfloat16),
        "exp",
        scatter_dimension=0,
        tiled=True,
    ).astype(jnp.float32)
    residual = hidden_in.astype(jnp.float32) + attn_out
    mixed = residual.astype(jnp.bfloat16)
    norm_scale = lax.rsqrt(jnp.mean(residual * residual, axis=1, keepdims=True) + 1e-06)
    normed = (residual * norm_scale * norm_gain).astype(jnp.bfloat16)
    slot_count = n_exp * CAP
    live = jnp.arange(token_rows, dtype=jnp.int32) < live_counts[0]
    active = (expert_ids < n_exp) & live[:, None]
    onehot = (
        (expert_ids[..., None] == jnp.arange(n_exp, dtype=jnp.int32)) & active[..., None]
    ).astype(jnp.int32)
    onehot = onehot.reshape(token_rows * TOPK, n_exp)
    earlier = jnp.cumsum(onehot, axis=0) - onehot
    rank = jnp.sum(earlier * onehot, axis=1).reshape(token_rows, TOPK)
    slot = jnp.where(active, expert_ids * CAP + rank, -1)
    pair_hit = slot[..., None] == jnp.arange(slot_count, dtype=jnp.int32)
    dispatch = jnp.any(pair_hit, axis=1).astype(jnp.bfloat16)
    send = jnp.einsum("rs,rd->sd", dispatch, normed, preferred_element_type=jnp.float32).astype(
        jnp.bfloat16
    )
    send = send.reshape(n_exp, CAP, D)
    route_weights = gate_fixed.astype(jnp.float32) / 4096.0
    combine = jnp.sum(pair_hit.astype(jnp.float32) * route_weights[..., None], axis=1)
    copies = jnp.broadcast_to(send[None], (n_ctx, n_exp, CAP, D)).reshape(n_ctx * n_exp, CAP, D)
    rows3 = lax.all_to_all(copies, ("ctx", "exp"), split_axis=0, concat_axis=0, tiled=True)
    flat_rows = rows3.reshape(-1, D)
    gate_part = jnp.dot(flat_rows, gate_proj[0], preferred_element_type=jnp.float32)
    up_part = jnp.dot(flat_rows, up_proj[0], preferred_element_type=jnp.float32)
    hidden = (jax.nn.silu(gate_part) * up_part).astype(jnp.bfloat16)
    partial_value = jnp.dot(hidden, down_proj[0], preferred_element_type=jnp.float32)
    partial_value = partial_value.reshape(rows3.shape[0], rows3.shape[1], D).astype(jnp.bfloat16)
    returned = lax.all_to_all(
        partial_value, ("ctx", "exp"), split_axis=0, concat_axis=0, tiled=True
    )
    expert_out = (
        returned.astype(jnp.float32).reshape(n_ctx, slot_count, D).sum(axis=0).astype(jnp.bfloat16)
    )
    expert_sum = jnp.dot(combine, expert_out.astype(jnp.float32), precision=lax.Precision.HIGHEST)
    return (mixed, expert_sum.astype(jnp.bfloat16))


def solution(mesh):
    in_specs = (
        P(("rep", "ctx", "exp"), None),
        P(("rep", "ctx"), "exp"),
        P(("rep", "ctx"), None),
        P(("rep", "ctx"), None),
        P("exp", None),
        P(),
        P(("rep", "ctx", "exp"), None),
        P(("rep", "ctx", "exp"), None),
        P(("rep", "ctx", "exp")),
        P("exp", None, "ctx"),
        P("exp", None, "ctx"),
        P("exp", "ctx", None),
    )
    out_specs = (P(("rep", "ctx", "exp"), None), P(("rep", "ctx", "exp"), None))
    sizes = mesh.shape
    fused = sizes["ctx"] == 1 and sizes["exp"] == N_EXP
    body = on_device_fused if fused else on_device_general
    return jax.shard_map(
        body, mesh=mesh, in_specs=in_specs, out_specs=out_specs, check_vma=False
    )
```

```python
import jax
import jax.numpy as jnp
from jax import lax
from jax.experimental import pallas as pl
from jax.experimental.pallas import tpu as pltpu
from jax.sharding import PartitionSpec as P

D = 4096
HEADS = 64
KV_HEADS = 4
HEAD_DIM = 128
TOPK = 8
CAP = 2


N_EXP = 16
ROWS = 32
SEQ = N_EXP * ROWS
HEAD_COLS = 512
FF = 1536
WIDE = 512
CHUNKS = D // WIDE
SLOTS = N_EXP * CAP
QBLOCK = 256
EARLY = 2
PIECES = 8
PAIR = 2 * WIDE
HALVES = 2


def fused_kernel(
    hidden_ref,
    q_ref,
    k_ref,
    v_ref,
    gain_ref,
    ids_ref,
    fixed_ref,
    live_ref,
    proj_hbm,
    gate_hbm,
    up_hbm,
    down_hbm,
    mixed_ref,
    sum_ref,
    proj,
    gate,
    up,
    down,
    attended,
    part,
    got1,
    got2,
    got3,
    gate_sum,
    up_sum,
    hid,
    send_rows,
    got_rows,
    send_back,
    got_back,
    send_norm,
    got_norm,
    load_sem,
    send1,
    recv1,
    send2,
    recv2,
    send3,
    recv3,
    send4,
    recv4,
    send5,
    recv5,
    send6,
    recv6,
):
    me = lax.axis_index("exp")
    x, y, z = me % 2, (me // 2) % 2, me // 4
    load_proj = pltpu.make_async_copy(proj_hbm, proj, load_sem.at[0])
    load_gate = pltpu.make_async_copy(gate_hbm.at[0], gate, load_sem.at[1])

    def load_up(piece):
        deep = slice(piece * PAIR, (piece + 1) * PAIR)
        return pltpu.make_async_copy(up_hbm.at[0, deep], up.at[deep], load_sem.at[2 + piece])

    def load_down(piece):
        deep = slice(piece * (FF // 4), (piece + 1) * (FF // 4))
        return pltpu.make_async_copy(down_hbm.at[0, deep], down.at[deep], load_sem.at[6 + piece])

    load_proj.start()
    load_gate.start()

    barrier = pltpu.get_barrier_semaphore()
    for step in range(1, N_EXP):
        pl.semaphore_signal(
            barrier,
            inc=1,
            device_id={"exp": (me + step) % N_EXP},
            device_id_type=pl.DeviceIdType.MESH,
        )

    kv = (me * (HEAD_COLS // HEAD_DIM)) // (HEADS // KV_HEADS)
    kv_cols = pl.ds(pl.multiple_of(kv * HEAD_DIM, HEAD_DIM), HEAD_DIM)
    scale = HEAD_DIM ** (-0.5)

    def attend(block):
        first = block * QBLOCK
        keys_seen = first + QBLOCK
        q_pos = first + lax.broadcasted_iota(jnp.int32, (QBLOCK, keys_seen), 0)
        k_pos = lax.broadcasted_iota(jnp.int32, (QBLOCK, keys_seen), 1)
        visible = k_pos <= q_pos
        for head in range(HEAD_COLS // HEAD_DIM):
            cols = slice(head * HEAD_DIM, (head + 1) * HEAD_DIM)
            scores = (
                lax.dot_general(
                    q_ref[first : first + QBLOCK, cols],
                    k_ref[:keys_seen, kv_cols],
                    (((1,), (1,)), ((), ())),
                    preferred_element_type=jnp.float32,
                )
                * scale
            )
            scores = jnp.where(visible, scores, -1e30)
            largest = jnp.max(scores, axis=1, keepdims=True)
            weights = jnp.exp(scores - largest)
            total = jnp.sum(weights, axis=1, keepdims=True)
            summed = jnp.dot(
                weights.astype(jnp.bfloat16),
                v_ref[:keys_seen, kv_cols],
                preferred_element_type=jnp.float32,
            )
            attended[first : first + QBLOCK, cols] = (summed / total).astype(jnp.bfloat16)

    x_peer, y_peer = me + 1 - 2 * x, me + 2 - 4 * y

    def places(odd):
        return (y, x, y_peer, x_peer) if odd else (x, y, x_peer, y_peer)

    def copy1(chunk, odd, half=None):
        a, _, peer, _ = places(odd)
        index = 0 if half is None else half
        planes = pl.ds(0, 4) if half is None else pl.ds(half * 2, 2)
        return pltpu.make_async_remote_copy(
            src_ref=part.at[chunk, 1 - a, :, planes],
            dst_ref=got1.at[chunk, :, planes],
            send_sem=send1.at[chunk, index],
            recv_sem=recv1.at[chunk, index],
            device_id={"exp": peer},
            device_id_type=pl.DeviceIdType.MESH,
        )

    def halves_of(pair):
        return (0, 1) if pair < EARLY else (None,)

    def copy2(chunk, odd):
        a, b, _, peer = places(odd)
        return pltpu.make_async_remote_copy(
            src_ref=part.at[chunk, a, 1 - b],
            dst_ref=got2.at[chunk],
            send_sem=send2.at[chunk],
            recv_sem=recv2.at[chunk],
            device_id={"exp": peer},
            device_id_type=pl.DeviceIdType.MESH,
        )

    def copy3(chunk, odd, step):
        a, b, _, _ = places(odd)
        other = (z + step) % 4
        return pltpu.make_async_remote_copy(
            src_ref=part.at[chunk, a, b, other],
            dst_ref=got3.at[chunk, step - 1],
            send_sem=send3.at[chunk, step - 1],
            recv_sem=recv3.at[chunk, step - 1],
            device_id={"exp": me + (other - z) * 4},
            device_id_type=pl.DeviceIdType.MESH,
        )

    def project(pair, half):
        lines = SEQ // 2
        for odd in (0, 1):
            chunk = pair * 2 + odd
            cols = slice(chunk * WIDE, (chunk + 1) * WIDE)
            for block in (0, 1) if half is None else (half,):
                product = jnp.dot(
                    attended[block * lines : (block + 1) * lines, :],
                    proj[:, cols],
                    preferred_element_type=jnp.float32,
                ).astype(jnp.bfloat16)
                for local in range(N_EXP // 2):
                    owner = block * (N_EXP // 2) + local
                    ox, oy, oz = owner % 2, (owner // 2) % 2, owner // 4
                    a, b = (oy, ox) if odd else (ox, oy)
                    part[chunk, a, b, oz] = product[local * ROWS : (local + 1) * ROWS, :]
            copy1(chunk, odd, half).start()

    def fold1(pair):
        for odd in (0, 1):
            chunk = pair * 2 + odd
            a = places(odd)[0]
            for half in halves_of(pair):
                copy1(chunk, odd, half).wait_recv()
            b = places(odd)[1]
            for c in range(4):
                part[chunk, a, 1 - b, c] = part[chunk, a, 1 - b, c] + got1[chunk, 1 - b, c]
            copy2(chunk, odd).start()
            for c in range(4):
                part[chunk, a, b, c] = part[chunk, a, b, c] + got1[chunk, b, c]

    def fold2(pair):
        for odd in (0, 1):
            chunk = pair * 2 + odd
            a, b, _, _ = places(odd)
            copy2(chunk, odd).wait_recv()
            for c in range(4):
                part[chunk, a, b, c] = part[chunk, a, b, c] + got2[chunk, c]
            for step in range(1, 4):
                copy3(chunk, odd, step).start()

    attend(0)
    load_proj.wait()
    pl.semaphore_wait(barrier, N_EXP - 1)
    for pair in range(EARLY):
        project(pair, 0)
    attend(1)
    for pair in range(EARLY):
        project(pair, 1)

    slot = lax.broadcasted_iota(jnp.int32, (SLOTS, ROWS), 0)
    row = lax.broadcasted_iota(jnp.int32, (SLOTS, ROWS), 1)
    weight = jnp.zeros((SLOTS, ROWS), jnp.int32)
    named = jnp.zeros((SLOTS, ROWS), jnp.float32)
    for k in range(TOPK):
        same = (ids_ref[k : k + 1, :] == slot // CAP) & (row < live_ref[0])
        weight = weight + jnp.where(same, fixed_ref[k : k + 1, :], 0)
        named = named + jnp.where(same, 1.0, 0.0)
    before = lax.broadcasted_iota(jnp.int32, (ROWS, ROWS), 0) < lax.broadcasted_iota(
        jnp.int32, (ROWS, ROWS), 1
    )
    earlier = jnp.dot(
        named.astype(jnp.bfloat16),
        jnp.where(before, 1.0, 0.0).astype(jnp.bfloat16),
        preferred_element_type=jnp.float32,
    )
    taken = (named > 0.5) & (jnp.abs(earlier - (slot % CAP).astype(jnp.float32)) < 0.5)
    dispatch_exact = jnp.where(taken, 1.0, 0.0)
    dispatch = dispatch_exact.astype(jnp.bfloat16)
    weight = jnp.where(taken, weight, 0)
    coarse = (weight // 64) * 64
    combine_hi = (coarse.astype(jnp.float32) / 4096.0).astype(jnp.bfloat16)
    combine_lo = ((weight - coarse).astype(jnp.float32) / 4096.0).astype(jnp.bfloat16)

    lines = SLOTS * PIECES
    per = CAP * PIECES
    i = lax.broadcasted_iota(jnp.int32, (lines, lines), 0)
    j = lax.broadcasted_iota(jnp.int32, (lines, lines), 1)
    to_work = jnp.where((i % SLOTS) * PIECES + i // SLOTS == j, 1.0, 0.0).astype(jnp.bfloat16)
    to_travel = jnp.where((j % SLOTS) * PIECES + j // SLOTS == i, 1.0, 0.0).astype(jnp.bfloat16)

    def reorder(matrix, value):
        return jnp.dot(matrix, value, preferred_element_type=jnp.float32).astype(jnp.bfloat16)

    def pieces_of(value):
        width = value.shape[1] // PIECES
        return jnp.concatenate(
            [value[:, p * width : (p + 1) * width] for p in range(PIECES)], axis=0
        )

    def whole_of(value):
        return jnp.concatenate(
            [value[p * SLOTS : (p + 1) * SLOTS, :] for p in range(PIECES)], axis=1
        )

    def exchange(source, target, send_sem, recv_sem, part_index, step):
        other = (me + step) % N_EXP
        return pltpu.make_async_remote_copy(
            src_ref=source.at[part_index, other],
            dst_ref=target.at[part_index, me],
            send_sem=send_sem.at[part_index, step - 1],
            recv_sem=recv_sem.at[part_index, step - 1],
            device_id={"exp": other},
            device_id_type=pl.DeviceIdType.MESH,
        )

    def there(pair, step):
        return exchange(send_rows, got_rows, send4, recv4, pair, step)

    def back(half, step):
        return exchange(send_back, got_back, send5, recv5, half, step)

    def norms(step):
        return exchange(send_norm, got_norm, send6, recv6, 0, step)

    def each_step(action):
        def body(step, _):
            action(step)
            return 0

        lax.fori_loop(1, N_EXP, body, 0)

    squares = [jnp.zeros((ROWS, 1), jnp.float32)]

    def final(pair):
        picked = []
        for odd in (0, 1):
            chunk = pair * 2 + odd
            a, b, _, _ = places(odd)
            for step in range(1, 4):
                copy3(chunk, odd, step).wait_recv()
            cols = slice(chunk * WIDE, (chunk + 1) * WIDE)
            total = part[chunk, a, b, z].astype(jnp.float32)
            for step in range(3):
                total = total + got3[chunk, step].astype(jnp.float32)
            total = total + hidden_ref[:, cols].astype(jnp.float32)
            mixed_ref[:, cols] = total.astype(jnp.bfloat16)
            squares[0] = squares[0] + jnp.sum(total * total, axis=1, keepdims=True)
            gained = (total * gain_ref[:, cols]).astype(jnp.bfloat16)
            picked.append(reorder(dispatch, gained))
        ordered = reorder(to_travel, pieces_of(jnp.concatenate(picked, axis=1)))
        for e in range(N_EXP):
            send_rows[pair, e] = ordered[e * per : (e + 1) * per, :]
        each_step(lambda step: there(pair, step).start())
        got_rows[pair, me] = send_rows[pair, me]

    def send_norms():
        norm = lax.rsqrt(squares[0] / D + 1e-06)
        wide = jnp.broadcast_to(norm, (ROWS, 128))
        slot_norm = jnp.dot(
            dispatch_exact, wide, precision=lax.Precision.HIGHEST, preferred_element_type=jnp.float32
        )
        line = lax.broadcasted_iota(jnp.int32, (N_EXP * 8, SLOTS), 0)
        source = lax.broadcasted_iota(jnp.int32, (N_EXP * 8, SLOTS), 1)
        spread = jnp.where((line // 8) * CAP + line % CAP == source, 1.0, 0.0)
        tiles = jnp.dot(
            spread, slot_norm, precision=lax.Precision.HIGHEST, preferred_element_type=jnp.float32
        )
        for e in range(N_EXP):
            send_norm[0, e] = tiles[e * 8 : (e + 1) * 8, :]
        each_step(lambda step: norms(step).start())
        got_norm[0, me] = send_norm[0, me]

    def receive_norms():
        each_step(lambda step: norms(step).wait_recv())
        line = lax.broadcasted_iota(jnp.int32, (SLOTS, N_EXP * 8), 1)
        target = lax.broadcasted_iota(jnp.int32, (SLOTS, N_EXP * 8), 0)
        gather = jnp.where((target // CAP) * 8 + target % CAP == line, 1.0, 0.0)
        return jnp.dot(
            gather,
            got_norm[0].reshape(N_EXP * 8, 128),
            precision=lax.Precision.HIGHEST,
            preferred_element_type=jnp.float32,
        )[:, :1]

    def expert_in(pair):
        if pair == 0:
            load_gate.wait()
        load_up(pair).wait()
        each_step(lambda step: there(pair, step).wait_recv())
        tokens = whole_of(reorder(to_work, got_rows[pair].reshape(lines, PAIR // PIECES)))
        deep = slice(pair * PAIR, (pair + 1) * PAIR)
        for block in range(FF // 512):
            cols = slice(block * 512, (block + 1) * 512)
            for weights_in, sums in ((gate, gate_sum), (up, up_sum)):
                term = jnp.dot(tokens, weights_in[deep, cols], preferred_element_type=jnp.float32)
                sums[:, cols] = term if pair == 0 else sums[:, cols] + term

    load_up(0).start()
    fold1(0)
    project(2, None)
    load_up(1).start()
    fold1(1)
    fold2(0)
    load_up(2).start()
    project(3, None)
    load_up(3).start()
    fold1(2)
    fold2(1)
    load_down(0).start()
    final(0)
    load_down(1).start()
    fold1(3)
    fold2(2)
    load_down(2).start()
    final(1)
    load_down(3).start()
    expert_in(0)
    final(2)
    fold2(3)
    expert_in(1)
    final(3)
    send_norms()
    expert_in(2)
    expert_in(3)
    slot_scale = receive_norms()
    for block in range(FF // 512):
        cols = slice(block * 512, (block + 1) * 512)
        gate_part = gate_sum[:, cols] * slot_scale
        up_part = up_sum[:, cols] * slot_scale
        hid[:, cols] = (gate_part / (1.0 + jnp.exp(-gate_part)) * up_part).astype(jnp.bfloat16)

    for piece in range(4):
        load_down(piece).wait()
    width = D // HALVES
    for half in range(HALVES):
        partial_rows = []
        for block in range(width // WIDE):
            first = half * width + block * WIDE
            partial_rows.append(
                jnp.dot(
                    hid[...], down[:, first : first + WIDE], preferred_element_type=jnp.float32
                ).astype(jnp.bfloat16)
            )
        ordered = reorder(to_travel, pieces_of(jnp.concatenate(partial_rows, axis=1)))
        for e in range(N_EXP):
            send_back[half, e] = ordered[e * per : (e + 1) * per, :]
        for step in range(1, N_EXP):
            back(half, step).start()
        got_back[half, me] = send_back[half, me]
    for half in range(HALVES):
        each_step(lambda step: back(half, step).wait_recv())
        returned = whole_of(reorder(to_work, got_back[half].reshape(lines, width // PIECES)))
        over = (((0,), (0,)), ((), ()))
        sum_ref[:, half * width : (half + 1) * width] = (
            lax.dot_general(combine_hi, returned, over, preferred_element_type=jnp.float32)
            + lax.dot_general(combine_lo, returned, over, preferred_element_type=jnp.float32)
        ).astype(jnp.bfloat16)

    for pair in range(CHUNKS // 2):
        for odd in (0, 1):
            chunk = pair * 2 + odd
            for half in halves_of(pair):
                copy1(chunk, odd, half).wait_send()
            copy2(chunk, odd).wait_send()
            for step in range(1, 4):
                copy3(chunk, odd, step).wait_send()
        each_step(lambda step: there(pair, step).wait_send())
    each_step(lambda step: norms(step).wait_send())
    for half in range(HALVES):
        each_step(lambda step: back(half, step).wait_send())


def on_device_fused(
    hidden_in,
    queries,
    keys,
    values,
    out_proj,
    norm_gain,
    expert_ids,
    gate_fixed,
    live_counts,
    gate_proj,
    up_proj,
    down_proj,
):
    bf16 = jnp.bfloat16
    dma = pltpu.SemaphoreType.DMA
    vmem = pl.BlockSpec(memory_space=pltpu.VMEM)
    hbm = pl.BlockSpec(memory_space=pl.ANY)
    going = pltpu.VMEM((D // PAIR, N_EXP, CAP * PIECES, PAIR // PIECES), bf16)
    coming = pltpu.VMEM((HALVES, N_EXP, CAP * PIECES, D // HALVES // PIECES), bf16)
    norm_tiles = pltpu.VMEM((1, N_EXP, 8, 128), jnp.float32)
    return pl.pallas_call(
        fused_kernel,
        out_shape=(pltpu.VMEM((ROWS, D), bf16), pltpu.VMEM((ROWS, D), bf16)),
        in_specs=[vmem] * 7 + [pl.BlockSpec(memory_space=pltpu.SMEM)] + [hbm] * 4,
        out_specs=(vmem, vmem),
        scratch_shapes=[
            pltpu.VMEM((HEAD_COLS, D), bf16),
            pltpu.VMEM((D, FF), bf16),
            pltpu.VMEM((D, FF), bf16),
            pltpu.VMEM((FF, D), bf16),
            pltpu.VMEM((SEQ, HEAD_COLS), bf16),
            pltpu.VMEM((CHUNKS, 2, 2, 4, ROWS, WIDE), bf16),
            pltpu.VMEM((CHUNKS, 2, 4, ROWS, WIDE), bf16),
            pltpu.VMEM((CHUNKS, 4, ROWS, WIDE), bf16),
            pltpu.VMEM((CHUNKS, 3, ROWS, WIDE), bf16),
            pltpu.VMEM((SLOTS, FF), jnp.float32),
            pltpu.VMEM((SLOTS, FF), jnp.float32),
            pltpu.VMEM((SLOTS, FF), bf16),
            going,
            going,
            coming,
            coming,
            norm_tiles,
            norm_tiles,
            dma((10,)),
            dma((CHUNKS, 2)),
            dma((CHUNKS, 2)),
            dma((CHUNKS,)),
            dma((CHUNKS,)),
            dma((CHUNKS, 3)),
            dma((CHUNKS, 3)),
            dma((D // PAIR, N_EXP - 1)),
            dma((D // PAIR, N_EXP - 1)),
            dma((HALVES, N_EXP - 1)),
            dma((HALVES, N_EXP - 1)),
            dma((1, N_EXP - 1)),
            dma((1, N_EXP - 1)),
        ],
        compiler_params=pltpu.CompilerParams(
            collective_id=0, has_side_effects=True, vmem_limit_bytes=56 * 2**20
        ),
        name="decoder_layer",
    )(
        hidden_in,
        queries,
        keys,
        values,
        norm_gain.reshape(1, D),
        expert_ids.T,
        gate_fixed.T,
        live_counts,
        out_proj,
        gate_proj,
        up_proj,
        down_proj,
    )


def on_device_general(
    hidden_in,
    queries,
    keys,
    values,
    out_proj,
    norm_gain,
    expert_ids,
    gate_fixed,
    live_counts,
    gate_proj,
    up_proj,
    down_proj,
):
    n_ctx = lax.axis_size("ctx")
    n_exp = lax.axis_size("exp")
    seq_rows = queries.shape[0]
    local_heads = queries.shape[1] // HEAD_DIM
    group = HEADS // KV_HEADS
    kv_index = lax.axis_index("exp") * local_heads // group
    key_head = lax.dynamic_slice_in_dim(keys, kv_index * HEAD_DIM, HEAD_DIM, 1)
    value_head = lax.dynamic_slice_in_dim(values, kv_index * HEAD_DIM, HEAD_DIM, 1)
    query_heads = queries.reshape(seq_rows, local_heads, HEAD_DIM).transpose(1, 0, 2)
    query_pos = lax.axis_index("ctx") * seq_rows + jnp.arange(seq_rows, dtype=jnp.int32)
    scale = HEAD_DIM ** (-0.5)

    def update(carry, key_block, value_block, first):
        running, total, accum = carry
        scores = (
            jnp.einsum("hqd,kd->hqk", query_heads, key_block, preferred_element_type=jnp.float32)
            * scale
        )
        key_pos = first + jnp.arange(seq_rows, dtype=jnp.int32)
        visible = (key_pos[None, :] <= query_pos[:, None])[None]
        scores = jnp.where(visible, scores, -1e30)
        newest = jnp.maximum(running, jnp.max(scores, axis=2))
        weights = jnp.where(visible, jnp.exp(scores - newest[..., None]), 0.0)
        factor = jnp.exp(running - newest)
        total = total * factor + jnp.sum(weights, axis=2)
        accum = accum * factor[..., None] + jnp.einsum(
            "hqk,kd->hqd",
            weights.astype(jnp.bfloat16),
            value_block,
            preferred_element_type=jnp.float32,
        )
        return (newest, total, accum)

    start_state = (
        jnp.full((local_heads, seq_rows), -1e30, jnp.float32),
        jnp.zeros((local_heads, seq_rows), jnp.float32),
        jnp.zeros((local_heads, seq_rows, HEAD_DIM), jnp.float32),
    )
    carry = start_state
    key_piece = lax.all_gather(key_head, "ctx", axis=0, tiled=True)
    value_piece = lax.all_gather(value_head, "ctx", axis=0, tiled=True)
    blocks = key_piece.shape[0] // seq_rows
    key_blocks = key_piece.reshape(blocks, seq_rows, HEAD_DIM)
    value_blocks = value_piece.reshape(blocks, seq_rows, HEAD_DIM)
    firsts = jnp.arange(blocks, dtype=jnp.int32) * seq_rows

    def step(state, inputs):
        key_block, value_block, first = inputs
        state = update(state, key_block, value_block, first)
        return (state, None)

    carry, _ = lax.scan(step, carry, (key_blocks, value_blocks, firsts))
    running, total, accum = carry
    attended = (
        (accum / total[..., None])
        .astype(jnp.bfloat16)
        .transpose(1, 0, 2)
        .reshape(seq_rows, local_heads * HEAD_DIM)
    )
    token_rows = hidden_in.shape[0]
    attn_out = lax.psum_scatter(
        jnp.dot(attended, out_proj, preferred_element_type=jnp.float32).astype(jnp.bfloat16),
        "exp",
        scatter_dimension=0,
        tiled=True,
    ).astype(jnp.float32)
    residual = hidden_in.astype(jnp.float32) + attn_out
    mixed = residual.astype(jnp.bfloat16)
    norm_scale = lax.rsqrt(jnp.mean(residual * residual, axis=1, keepdims=True) + 1e-06)
    normed = (residual * norm_scale * norm_gain).astype(jnp.bfloat16)
    slot_count = n_exp * CAP
    live = jnp.arange(token_rows, dtype=jnp.int32) < live_counts[0]
    active = (expert_ids < n_exp) & live[:, None]
    onehot = (
        (expert_ids[..., None] == jnp.arange(n_exp, dtype=jnp.int32)) & active[..., None]
    ).astype(jnp.int32)
    onehot = onehot.reshape(token_rows * TOPK, n_exp)
    earlier = jnp.cumsum(onehot, axis=0) - onehot
    rank = jnp.sum(earlier * onehot, axis=1).reshape(token_rows, TOPK)
    slot = jnp.where(active, expert_ids * CAP + rank, -1)
    pair_hit = slot[..., None] == jnp.arange(slot_count, dtype=jnp.int32)
    dispatch = jnp.any(pair_hit, axis=1).astype(jnp.bfloat16)
    send = jnp.einsum("rs,rd->sd", dispatch, normed, preferred_element_type=jnp.float32).astype(
        jnp.bfloat16
    )
    send = send.reshape(n_exp, CAP, D)
    route_weights = gate_fixed.astype(jnp.float32) / 4096.0
    combine = jnp.sum(pair_hit.astype(jnp.float32) * route_weights[..., None], axis=1)
    copies = jnp.broadcast_to(send[None], (n_ctx, n_exp, CAP, D)).reshape(n_ctx * n_exp, CAP, D)
    rows3 = lax.all_to_all(copies, ("ctx", "exp"), split_axis=0, concat_axis=0, tiled=True)
    flat_rows = rows3.reshape(-1, D)
    gate_part = jnp.dot(flat_rows, gate_proj[0], preferred_element_type=jnp.float32)
    up_part = jnp.dot(flat_rows, up_proj[0], preferred_element_type=jnp.float32)
    hidden = (jax.nn.silu(gate_part) * up_part).astype(jnp.bfloat16)
    partial_value = jnp.dot(hidden, down_proj[0], preferred_element_type=jnp.float32)
    partial_value = partial_value.reshape(rows3.shape[0], rows3.shape[1], D).astype(jnp.bfloat16)
    returned = lax.all_to_all(
        partial_value, ("ctx", "exp"), split_axis=0, concat_axis=0, tiled=True
    )
    expert_out = (
        returned.astype(jnp.float32).reshape(n_ctx, slot_count, D).sum(axis=0).astype(jnp.bfloat16)
    )
    expert_sum = jnp.dot(combine, expert_out.astype(jnp.float32), precision=lax.Precision.HIGHEST)
    return (mixed, expert_sum.astype(jnp.bfloat16))


def solution(mesh):
    in_specs = (
        P(("rep", "ctx", "exp"), None),
        P(("rep", "ctx"), "exp"),
        P(("rep", "ctx"), None),
        P(("rep", "ctx"), None),
        P("exp", None),
        P(),
        P(("rep", "ctx", "exp"), None),
        P(("rep", "ctx", "exp"), None),
        P(("rep", "ctx", "exp")),
        P("exp", None, "ctx"),
        P("exp", None, "ctx"),
        P("exp", "ctx", None),
    )
    out_specs = (P(("rep", "ctx", "exp"), None), P(("rep", "ctx", "exp"), None))
    sizes = mesh.shape
    fused = sizes["ctx"] == 1 and sizes["exp"] == N_EXP
    body = on_device_fused if fused else on_device_general
    return jax.shard_map(
        body, mesh=mesh, in_specs=in_specs, out_specs=out_specs, check_vma=False
    )
```
